128 devices in a mesh: row: 8 (over y, z_lo), col: 16 (over z_hi, x, core).
Axes of the slice: x: 4, y: 4, z: 4 (z_hi: 2, z_lo: 2; z = z_hi * 2 + z_lo), core: 2. Of those that a mesh axis runs over, the one named last changes fastest.
Arguments:
- value: bfloat16 [1024, 1024, 128], P('row', 'col'), may hold values from -6 to 6
- gate: bfloat16 [1024, 1024, 128], P('row', 'col'), may hold values from -6 to 6
- filter_real: float32 [1024, 1024, 128], P(None, ('row', 'col')), may hold values from -6 to 6
- filter_imag: float32 [1024, 1024, 128], P(None, ('row', 'col')), may hold values from -6 to 6
- skip: float32 [128], replicated, may hold values from -4 to 4
Outputs:
- gated: bfloat16 [1024, 1024, 128], P('row', 'col')
The draws below stay inside these ranges and needn't reach their ends.
All inputs are finite; a program needn't handle non-finite values.
Results may differ from the reference program's by a relative error of at most 0.001.
Values may be sent and summed in bfloat16 or wider, within the bound.
No kernel may reach another device: no remote copies, remote signals or barrier semaphores. Data moves between devices by JAX's collectives and lax.ppermute only.
A program may use at most 192 MiB of HBM per device.

```python
import math
import jax
import jax.numpy as jnp
from jax import lax

GRID_P = 1024
GRID_Q = 1024
CH = 128


def steps_of(rng, dims, shards, low, largest):
    def one(position, shards_of):
        steps = jax.random.uniform(jax.random.fold_in(jax.random.fold_in(rng, 6), position), (shards_of,), jnp.float32, low / len(shards), largest / len(shards))
        return jnp.repeat(jnp.exp(steps), dims[position] // shards_of).reshape((-1,) + (1,) * (len(dims) - position - 1))

    factor_of = one(*shards[0])
    for cut in shards[1:]:
        factor_of = factor_of * one(*cut)
    return factor_of


def normal_values(key, extent, scale, bound, shards=(), kind=jnp.bfloat16):
    entries = scale * jax.random.normal(key, extent, jnp.float32)
    if shards:
        entries = entries * steps_of(key, extent, shards, -0.22, 0.18)
    return jnp.clip(entries, -bound, bound).astype(kind)


def setup_inputs(seed: int = 0) -> dict:
    key_list = jax.random.split(jax.random.key(seed), 6)
    return {
        "value": normal_values(key_list[0], (GRID_P, GRID_Q, CH), 1.0, 6.0, ((0, 8), (1, 16))),
        "gate": normal_values(key_list[1], (GRID_P, GRID_Q, CH), 1.0, 6.0, ((0, 8), (1, 16))),
        "filter_real": normal_values(key_list[2], (GRID_Q, GRID_P, CH), 1.0, 6.0, ((1, 128),), jnp.float32),
        "filter_imag": normal_values(key_list[3], (GRID_Q, GRID_P, CH), 1.0, 6.0, ((1, 128),), jnp.float32),
        "skip": normal_values(key_list[4], (CH,), 1.0, 4.0, (), jnp.float32),
    }


def reference(value, gate, filter_real, filter_imag, skip):
    positions = GRID_P * GRID_Q
    block_size = math.gcd(CH, 16)
    groups = CH // block_size
    flat_value = value.reshape(positions, CH)
    flat_gate = gate.reshape(positions, CH)
    flat_real = filter_real.reshape(positions, CH)
    flat_imag = filter_imag.reshape(positions, CH)

    def one_block(group_index):
        first_channel = (group_index * block_size).astype(jnp.int32)
        part_value = lax.dynamic_slice_in_dim(flat_value, first_channel, block_size, 1).astype(jnp.float32)
        part_gate = lax.dynamic_slice_in_dim(flat_gate, first_channel, block_size, 1).astype(jnp.float32)
        part_real = lax.dynamic_slice_in_dim(flat_real, first_channel, block_size, 1)
        part_imag = lax.dynamic_slice_in_dim(flat_imag, first_channel, block_size, 1)
        part_skip = lax.dynamic_slice_in_dim(skip, first_channel, block_size, 0)
        spectrum = jnp.fft.fft(part_value, axis=0)
        response = lax.complex(part_real, part_imag)
        convolved = jnp.real(jnp.fft.ifft(spectrum * response, axis=0))
        result = part_gate * (convolved + part_skip * part_value)
        return result.astype(jnp.bfloat16)

    blocks = lax.map(one_block, jnp.arange(groups, dtype=jnp.int32))
    return jnp.moveaxis(blocks, 0, 1).reshape(GRID_P, GRID_Q, CH)
```

```python
import math

import jax
import jax.numpy as jnp
import numpy as np
from jax import lax
from jax.experimental import pallas as pl
from jax.experimental.pallas import tpu as pltpu
from jax.sharding import PartitionSpec as P

half_root = math.sqrt(0.5)
span = 124.0
ln2 = math.log(2.0)
f32 = jnp.float32
bf16 = jnp.bfloat16
vmem_bytes = 56 * 1024 * 1024


def turn(x, sign):
    re, im = x
    return (-im, re) if sign > 0 else (im, -re)


def add(x, y):
    return (x[0] + y[0], x[1] + y[1])


def sub(x, y):
    return (x[0] - y[0], x[1] - y[1])


def scale_root(x, index, period, sign):
    index %= period
    if index == 0:
        return x
    if 4 * index == period:
        return turn(x, sign)
    if 2 * index == period:
        return (-x[0], -x[1])
    re, im = x
    if 8 * index == period:
        if sign > 0:
            return ((re - im) * half_root, (im + re) * half_root)
        return ((re + im) * half_root, (im - re) * half_root)
    if 8 * index == 3 * period:
        if sign > 0:
            return ((re + im) * -half_root, (re - im) * half_root)
        return ((im - re) * half_root, (re + im) * -half_root)
    angle = 2.0 * math.pi * index / period
    c, s = math.cos(angle), sign * math.sin(angle)
    return (re * c - im * s, re * s + im * c)


def times(x, c, s):
    re, im = x
    return (re * c - im * s, re * s + im * c)


def times_conj(x, c, s):
    re, im = x
    return (re * c + im * s, im * c - re * s)


def dft4(y, sign):
    t0, t1 = add(y[0], y[2]), sub(y[0], y[2])
    t2, t3 = add(y[1], y[3]), turn(sub(y[1], y[3]), sign)
    return [add(t0, t2), add(t1, t3), sub(t0, t2), sub(t1, t3)]


def dft8(x, sign):
    even = dft4([add(x[k], x[k + 4]) for k in range(4)], sign)
    odd = dft4([scale_root(sub(x[k], x[k + 4]), k, 8, sign) for k in range(4)], sign)
    return [even[0], odd[0], even[1], odd[1], even[2], odd[2], even[3], odd[3]]


def dft16(x, sign):
    first = [dft4([x[4 * a + b] for a in range(4)], sign) for b in range(4)]
    out = [None] * 16
    for c in range(4):
        last = dft4([scale_root(first[b][c], b * c, 16, sign) for b in range(4)], sign)
        for e in range(4):
            out[c + 4 * e] = last[e]
    return out


def get(re_ref, im_ref, i, at):
    return (re_ref[i, at], im_ref[i, at])


def put(re_ref, im_ref, i, at, x):
    re_ref[i, at] = x[0]
    im_ref[i, at] = x[1]


def transform_128(re_ref, im_ref, i, sign):
    for b in range(16):
        x = dft8([get(re_ref, im_ref, i, 16 * a + b) for a in range(8)], sign)
        for c in range(8):
            put(re_ref, im_ref, i, 16 * c + b, scale_root(x[c], b * c, 128, sign))
    for c in range(8):
        x = dft16([get(re_ref, im_ref, i, 16 * c + b) for b in range(16)], sign)
        for e in range(16):
            put(re_ref, im_ref, i, 16 * c + e, x[e])


def untransform_128(re_ref, im_ref, i, sign):
    for c in range(8):
        x = dft16([get(re_ref, im_ref, i, 16 * c + e) for e in range(16)], sign)
        for b in range(16):
            put(re_ref, im_ref, i, 16 * c + b, scale_root(x[b], b * c, 128, sign))
    for b in range(16):
        x = dft8([get(re_ref, im_ref, i, 16 * c + b) for c in range(8)], sign)
        for a in range(8):
            put(re_ref, im_ref, i, 16 * a + b, x[a])


def place(k):
    return 16 * (k % 8) + k // 8


def encode(blocks, store):
    top = jnp.abs(blocks[0])
    for x in blocks[1:]:
        top = jnp.maximum(top, jnp.abs(x))
    scale = jnp.maximum(top * (1.0 / span), 1e-35).astype(bf16)
    inverse = 1.0 / scale.astype(f32)
    for k in range(8):
        pair = jnp.concatenate([blocks[2 * k] * inverse, blocks[2 * k + 1] * inverse], axis=0)
        store(slice(16 * k, 16 * k + 16), jnp.exp2(pair).astype(bf16))
    store(slice(128, 136), scale)


def decode_scale(rows):
    return rows.astype(f32) * (1.0 / ln2)


def decode_pair(rows):
    logs = jnp.log(rows.astype(f32))
    return logs[0:8], logs[8:16]


def forward_kernel(x_ref, table_ref, out_ref, re_ref, im_ref):
    def first(pair, carry):
        both = [x_ref[64 * r + pair].astype(f32) for r in range(8)]
        for odd in range(2):
            m = 2 * pair + odd
            x = [v[8 * odd : 8 * odd + 8] for v in both]
            s = [x[k] + x[k + 4] for k in range(4)]
            d = [x[k] - x[k + 4] for k in range(4)]
            s02, s13 = s[0] + s[2], s[1] + s[3]
            re_ref[0, m] = s02 + s13
            im_ref[0, m] = jnp.zeros_like(s02)
            low, high = (d[1] - d[3]) * half_root, (d[1] + d[3]) * half_root
            rows = [None, (d[0] + low, -d[2] - high), (s[0] - s[2], s[3] - s[1]), (d[0] - low, d[2] - high)]
            for i in range(1, 4):
                put(re_ref, im_ref, i, m, times(rows[i], table_ref[16 * m + i], table_ref[16 * m + 8 + i]))
            mid = s02 - s13
            put(re_ref, im_ref, 4, m, (mid * table_ref[16 * m + 4], mid * table_ref[16 * m + 12]))
        return carry

    lax.fori_loop(0, 64, first, 0)

    def second(i, carry):
        transform_128(re_ref, im_ref, i, -1)
        return carry

    lax.fori_loop(0, 5, second, 0)

    def third(d, carry):
        here, there = place(d), place(127 - d)
        blocks = []
        for i in range(5):
            blocks += [re_ref[i, here], im_ref[i, here]]
        for i in range(5, 8):
            blocks += [re_ref[8 - i, there], -im_ref[8 - i, there]]

        def store(rows, v):
            out_ref[d, rows, :] = v

        encode(blocks, store)
        return carry

    lax.fori_loop(0, 128, third, 0)


def middle_kernel(x_ref, twist_cos, twist_sin, filter_real, filter_imag, table_ref, out_ref,
                  re_ref, im_ref, tc_ref, ts_ref, fr_ref, fi_ref, sems):
    copies = [
        pltpu.make_async_copy(src, dst, sems.at[k])
        for k, (src, dst) in enumerate(
            [(twist_cos, tc_ref), (twist_sin, ts_ref), (filter_real, fr_ref), (filter_imag, fi_ref)]
        )
    ]
    for c in copies:
        c.start()
    copies[0].wait()
    copies[1].wait()

    def first(src, carry):
        a = 8 * (src % 16) + src // 16
        scale = decode_scale(x_ref[src, 128:136, :])
        for i in range(8):
            x = decode_pair(x_ref[src, 16 * i : 16 * i + 16, :])
            y = times(x, scale * tc_ref[a, i], scale * ts_ref[a, i])
            put(re_ref, im_ref, i, a, y)
        return carry

    lax.fori_loop(0, 128, first, 0)

    def second(i, carry):
        transform_128(re_ref, im_ref, i, -1)
        return carry

    lax.fori_loop(0, 8, second, 0)
    copies[2].wait()
    copies[3].wait()

    def third(at, carry):
        b = at // 16 + 8 * (at % 16)
        re = jnp.stack([re_ref[i, at] for i in range(8)])
        im = jnp.stack([im_ref[i, at] for i in range(8)])
        re, im = jnp.swapaxes(re, 0, 1), jnp.swapaxes(im, 0, 1)
        x = [(re[0], im[0])]
        for j in range(1, 8):
            x.append(times((re[j], im[j]), table_ref[16 * b + j], table_ref[16 * b + 8 + j]))
        x = dft8(x, -1)
        y = [times(x[e], fr_ref[b + 128 * e], fi_ref[b + 128 * e]) for e in range(8)]
        y = dft8(y, 1)
        for j in range(1, 8):
            y[j] = times_conj(y[j], table_ref[16 * b + j], table_ref[16 * b + 8 + j])
        re = jnp.swapaxes(jnp.stack([v[0] for v in y]), 0, 1)
        im = jnp.swapaxes(jnp.stack([v[1] for v in y]), 0, 1)
        for i in range(8):
            put(re_ref, im_ref, i, at, (re[i], im[i]))
        return carry

    lax.fori_loop(0, 128, third, 0)

    def fourth(i, carry):
        untransform_128(re_ref, im_ref, i, 1)
        return carry

    lax.fori_loop(0, 8, fourth, 0)

    def fifth(src, carry):
        a = 8 * (src % 16) + src // 16
        blocks = []
        for i in range(8):
            blocks += times_conj(get(re_ref, im_ref, i, a), tc_ref[a, i], ts_ref[a, i])

        def store(rows, v):
            out_ref[src, rows, :] = v

        encode(blocks, store)
        return carry

    lax.fori_loop(0, 128, fifth, 0)


def backward_kernel(x_ref, table_ref, out_ref, re_ref, im_ref, conv_ref):
    def first(d, carry):
        sides = []
        for src in (d, 127 - d):
            scale = decode_scale(x_ref[src, 128:136, :])
            side = []
            for i in range(8):
                lre, lim = decode_pair(x_ref[src, 16 * i : 16 * i + 16, :])
                side.append((lre * scale, lim * scale))
            sides.append(side)
        for k, src in enumerate((d, 127 - d)):
            near, far = sides[k], sides[1 - k]
            put(re_ref, im_ref, 0, src, near[0])
            put(re_ref, im_ref, 4, src, near[4])
            for i in range(1, 4):
                put(re_ref, im_ref, i, src, (near[i][0] + far[8 - i][0], near[i][1] - far[8 - i][1]))
        return carry

    lax.fori_loop(0, 64, first, 0)

    def second(i, carry):
        transform_128(re_ref, im_ref, i, 1)
        return carry

    lax.fori_loop(0, 5, second, 0)

    def third(at, carry):
        m = at // 16 + 8 * (at % 16)
        u0 = re_ref[0, at]
        z = [times_conj(get(re_ref, im_ref, i, at), table_ref[16 * m + i], table_ref[16 * m + 8 + i]) for i in range(1, 4)]
        re4, im4 = get(re_ref, im_ref, 4, at)
        u4 = re4 * table_ref[16 * m + 4] + im4 * table_ref[16 * m + 12]
        (x1, y1), (x2, y2), (x3, y3) = z
        even, odd = u0 + u4, u0 - u4
        x13, y13 = x1 + x3, y1 - y3
        up, down = even + x2, even - x2
        conv_ref[0, m] = up + x13
        conv_ref[4, m] = up - x13
        conv_ref[2, m] = down - y13
        conv_ref[6, m] = down + y13
        aa, bb = (x1 - x3) * half_root, (y1 + y3) * half_root
        up, down = odd + y2, odd - y2
        diff, both = aa - bb, aa + bb
        conv_ref[1, m] = down + diff
        conv_ref[5, m] = down - diff
        conv_ref[3, m] = up - both
        conv_ref[7, m] = up + both
        return carry

    lax.fori_loop(0, 128, third, 0)

    def fourth(step, carry):
        r, g = step // 8, step % 8
        blocks = [conv_ref[r, 16 * g + k] * (1.0 / 1048576.0) for k in range(16)]

        def store(rows, v):
            out_ref[r, g, rows, :] = v

        encode(blocks, store)
        return carry

    lax.fori_loop(0, 64, fourth, 0)


def gate_kernel(x_ref, value_ref, gate_ref, skip_ref, out_ref):
    skip = skip_ref[0:1, :]

    def body(k, carry):
        start = pl.multiple_of(16 * k, 16)
        for pair in range(4):
            sides = []
            for r in (2 * pair, 2 * pair + 1):
                scale = decode_scale(x_ref[r, 0, 128:136, :])
                low, high = decode_pair(x_ref[r, 0, pl.ds(start, 16), :])
                sides.append((low * scale, high * scale))
            for odd in range(2):
                conv = jnp.concatenate([sides[0][odd], sides[1][odd]], axis=0)
                rows = slice(16 * pair, 16 * pair + 16)
                v = value_ref[2 * k + odd, rows, :].astype(f32)
                g = gate_ref[2 * k + odd, rows, :].astype(f32)
                out_ref[2 * k + odd, rows, :] = (g * (conv + skip * v)).astype(bf16)
        return carry

    lax.fori_loop(0, 8, body, 0)


def roots_table(period):
    m, i = np.arange(128)[:, None], np.arange(8)[None, :]
    angle = -2.0 * np.pi * (m * i % period) / period
    return np.concatenate([np.cos(angle), np.sin(angle)], axis=1).astype(np.float32).reshape(-1)


def twist_tables(device):
    shape = (128, 8, 8)
    q = 8 * lax.broadcasted_iota(jnp.int32, shape, 0) + lax.broadcasted_iota(jnp.int32, shape, 2)
    kp = 8 * device + lax.broadcasted_iota(jnp.int32, shape, 1)
    angle = (q * kp % 1048576).astype(f32) * (-2.0 * math.pi / 1048576.0)
    cosine, sine = lax.optimization_barrier((jnp.cos(angle), jnp.sin(angle)))
    wide = shape + (128,)
    return jnp.broadcast_to(cosine[..., None], wide), jnp.broadcast_to(sine[..., None], wide)


def vspec():
    return pl.BlockSpec(memory_space=pltpu.VMEM)


def sspec():
    return pl.BlockSpec(memory_space=pltpu.SMEM)


def aspec():
    return pl.BlockSpec(memory_space=pl.ANY)


def params():
    return pltpu.CompilerParams(vmem_limit_bytes=vmem_bytes)


def forward(columns, table):
    return pl.pallas_call(
        forward_kernel,
        out_shape=jax.ShapeDtypeStruct((128, 136, 128), bf16),
        in_specs=[vspec(), sspec()],
        out_specs=vspec(),
        scratch_shapes=[pltpu.VMEM((5, 128, 8, 128), f32)] * 2,
        compiler_params=params(),
        name="forward_columns",
    )(columns, table)


def middle(arrived, twist_cos, twist_sin, filter_real, filter_imag, table):
    return pl.pallas_call(
        middle_kernel,
        out_shape=jax.ShapeDtypeStruct((128, 136, 128), bf16),
        in_specs=[vspec()] + [aspec()] * 4 + [sspec()],
        out_specs=vspec(),
        scratch_shapes=[pltpu.VMEM((8, 128, 8, 128), f32)] * 2
        + [pltpu.VMEM((128, 8, 8, 128), f32)] * 2
        + [pltpu.VMEM((1024, 8, 128), f32)] * 2
        + [pltpu.SemaphoreType.DMA((4,))],
        compiler_params=params(),
        name="filter_rows",
    )(arrived, twist_cos, twist_sin, filter_real, filter_imag, table)


def backward(returned, table):
    return pl.pallas_call(
        backward_kernel,
        out_shape=jax.ShapeDtypeStruct((8, 8, 136, 128), bf16),
        in_specs=[vspec(), sspec()],
        out_specs=vspec(),
        scratch_shapes=[pltpu.VMEM((5, 128, 8, 128), f32)] * 2 + [pltpu.VMEM((8, 128, 8, 128), f32)],
        compiler_params=params(),
        name="backward_columns",
    )(returned, table)


def gating(settled, value, gate, skip):
    return pl.pallas_call(
        gate_kernel,
        grid=(8,),
        out_shape=jax.ShapeDtypeStruct((128, 64, 128), bf16),
        in_specs=[
            pl.BlockSpec((8, 1, 136, 128), lambda g: (0, g, 0, 0)),
            pl.BlockSpec((16, 64, 128), lambda g: (g, 0, 0)),
            pl.BlockSpec((16, 64, 128), lambda g: (g, 0, 0)),
            pl.BlockSpec((1, 128), lambda g: (0, 0)),
        ],
        out_specs=pl.BlockSpec((16, 64, 128), lambda g: (g, 0, 0)),
        compiler_params=params(),
        name="gating",
    )(settled, value, gate, skip.reshape(1, 128))


def convolve(value, gate, filter_real, filter_imag, skip):
    device = lax.axis_index("row") * 16 + lax.axis_index("col")
    table = jnp.asarray(roots_table(1024))
    pieces = value.reshape(128, 8, 8, 128)
    columns = lax.all_to_all(pieces, "row", split_axis=1, concat_axis=0, tiled=True)
    spectrum = forward(columns.reshape(512, 16, 128), table)
    twist_cos, twist_sin = twist_tables(device)
    arrived = lax.all_to_all(spectrum, ("row", "col"), split_axis=0, concat_axis=0, tiled=True)
    leaving = middle(arrived, twist_cos, twist_sin, filter_real, filter_imag, table)
    returned = lax.all_to_all(leaving, ("row", "col"), split_axis=0, concat_axis=0, tiled=True)
    convolved = backward(returned, table)
    settled = lax.all_to_all(convolved, "row", split_axis=0, concat_axis=0, tiled=True)
    return gating(settled, value, gate, skip)


def solution(mesh):
    return jax.shard_map(
        convolve,
        mesh=mesh,
        in_specs=(
            P("row", "col", None),
            P("row", "col", None),
            P(None, ("row", "col"), None),
            P(None, ("row", "col"), None),
            P(),
        ),
        out_specs=P("row", "col", None),
        check_vma=False,
    )
```

```python
import math

import jax
import jax.numpy as jnp
import numpy as np
from jax import lax
from jax.experimental import pallas as pl
from jax.experimental.pallas import tpu as pltpu
from jax.sharding import PartitionSpec as P

TM = 4
TE = 8
TD = 8
half_root = math.sqrt(0.5)
span = 124.0
ln2 = math.log(2.0)
f32 = jnp.float32
bf16 = jnp.bfloat16


def turn(x, sign):
    re, im = x
    return (-im, re) if sign > 0 else (im, -re)


def add(x, y):
    return (x[0] + y[0], x[1] + y[1])


def sub(x, y):
    return (x[0] - y[0], x[1] - y[1])


def scale_root(x, index, period, sign):
    index %= period
    if index == 0:
        return x
    if 4 * index == period:
        return turn(x, sign)
    if 2 * index == period:
        return (-x[0], -x[1])
    re, im = x
    if 8 * index == period:
        if sign > 0:
            return ((re - im) * half_root, (im + re) * half_root)
        return ((re + im) * half_root, (im - re) * half_root)
    if 8 * index == 3 * period:
        if sign > 0:
            return ((re + im) * -half_root, (re - im) * half_root)
        return ((im - re) * half_root, (re + im) * -half_root)
    angle = 2.0 * math.pi * index / period
    c, s = math.cos(angle), sign * math.sin(angle)
    return (re * c - im * s, re * s + im * c)


def times(x, c, s):
    re, im = x
    return (re * c - im * s, re * s + im * c)


def times_conj(x, c, s):
    re, im = x
    return (re * c + im * s, im * c - re * s)


def dft4(y, sign):
    t0, t1 = add(y[0], y[2]), sub(y[0], y[2])
    t2, t3 = add(y[1], y[3]), turn(sub(y[1], y[3]), sign)
    return [add(t0, t2), add(t1, t3), sub(t0, t2), sub(t1, t3)]


def dft8(x, sign):
    even = dft4([add(x[k], x[k + 4]) for k in range(4)], sign)
    odd = dft4([scale_root(sub(x[k], x[k + 4]), k, 8, sign) for k in range(4)], sign)
    return [even[0], odd[0], even[1], odd[1], even[2], odd[2], even[3], odd[3]]


def dft16(x, sign):
    first = [dft4([x[4 * a + b] for a in range(4)], sign) for b in range(4)]
    out = [None] * 16
    for c in range(4):
        last = dft4([scale_root(first[b][c], b * c, 16, sign) for b in range(4)], sign)
        for e in range(4):
            out[c + 4 * e] = last[e]
    return out


STR = 1032


def rows_of(i, at):
    start = i * STR + at * 8
    if STR % 8 == 0 and not isinstance(start, int):
        start = pl.multiple_of(start, 8)
    return pl.ds(start, 8)


def get(re_ref, im_ref, i, at):
    rows = rows_of(i, at)
    return (re_ref[rows, :], im_ref[rows, :])


def put(re_ref, im_ref, i, at, x):
    rows = rows_of(i, at)
    re_ref[rows, :] = x[0]
    im_ref[rows, :] = x[1]


def transform_128(re_ref, im_ref, i, sign):
    for b in range(16):
        x = dft8([get(re_ref, im_ref, i, 16 * a + b) for a in range(8)], sign)
        for c in range(8):
            put(re_ref, im_ref, i, 16 * c + b, scale_root(x[c], b * c, 128, sign))
    for c in range(8):
        x = dft16([get(re_ref, im_ref, i, 16 * c + b) for b in range(16)], sign)
        for e in range(16):
            put(re_ref, im_ref, i, 16 * c + e, x[e])


def repeat(count, step, together=1):
    def body(k, carry):
        for u in range(together):
            step(together * k + u)
        return carry

    lax.fori_loop(0, count // together, body, 0)


def place(k):
    return 16 * (k % 8) + k // 8


def encode(blocks, store):
    tops = [jnp.abs(x) for x in blocks]
    while len(tops) > 1:
        tops = [jnp.maximum(x, y) for x, y in zip(tops[::2], tops[1::2])] + tops[len(tops) // 2 * 2 :]
    scale = jnp.maximum(tops[0] * (1.0 / span), 1e-35).astype(bf16)
    inverse = 1.0 / scale.astype(f32)
    for k in range(len(blocks) // 2):
        pair = jnp.concatenate([blocks[2 * k] * inverse, blocks[2 * k + 1] * inverse], axis=0)
        store(slice(16 * k, 16 * k + 16), jnp.exp2(pair).astype(bf16))
    store(slice(8 * len(blocks), 8 * len(blocks) + 8), scale)


def decode_scale(rows):
    return rows.astype(f32) * (1.0 / ln2)


def decode_pair(rows):
    logs = jnp.log(rows.astype(f32))
    return logs[0:8], logs[8:16]


def forward_kernel(x_ref, table_ref, out_ref, re_ref, im_ref):
    def first(pair):
        both = [x_ref[64 * r + pair].astype(f32) for r in range(8)]
        for odd in range(2):
            m = 2 * pair + odd
            x = [v[8 * odd : 8 * odd + 8] for v in both]
            s = [x[k] + x[k + 4] for k in range(4)]
            d = [x[k] - x[k + 4] for k in range(4)]
            s02, s13 = s[0] + s[2], s[1] + s[3]
            put(re_ref, im_ref, 0, m, (s02 + s13, jnp.zeros_like(s02)))
            low, high = (d[1] - d[3]) * half_root, (d[1] + d[3]) * half_root
            rows = [None, (d[0] + low, -d[2] - high), (s[0] - s[2], s[3] - s[1]), (d[0] - low, d[2] - high)]
            for i in range(1, 4):
                put(re_ref, im_ref, i, m, times(rows[i], table_ref[16 * m + i], table_ref[16 * m + 8 + i]))
            mid = s02 - s13
            put(re_ref, im_ref, 4, m, (mid * table_ref[16 * m + 4], mid * table_ref[16 * m + 12]))

    repeat(64, first)

    def second(i):
        transform_128(re_ref, im_ref, i, -1)

    repeat(5, second)

    def third(d):
        blocks = []
        for i in range(5):
            blocks += get(re_ref, im_ref, i, place(d))

        def store(rows, v):
            out_ref[d, rows, :] = v

        encode(blocks, store)

    repeat(128, third, TE)


def lane(x, k):
    return jnp.broadcast_to(x[:, k : k + 1], (8, 128))


def filter_kernel(re_ref, im_ref, out_ref):
    for s in range(3):
        blocks = []
        for u in range(8):
            rows = pl.ds(64 * u + 7 - s, 8, stride=8)
            blocks += [re_ref[rows, :], im_ref[rows, :]]

        def store(rows, v):
            out_ref[0, s, rows, :] = v

        encode(blocks, store)


def prepare_kernel(re_ref, im_ref, code_ref, twist_ref, out_re, out_im, cos_ref, sin_ref, far_re, far_im):
    far_re[...] = jnp.zeros((512, 128), f32)
    far_im[...] = jnp.zeros((512, 128), f32)
    for s in range(3):
        scale = decode_scale(code_ref[0, s, 128:136, :])
        for u in range(8):
            lre, lim = decode_pair(code_ref[0, s, 16 * u : 16 * u + 16, :])
            rows = pl.ds(64 * u + s + 1, 8, stride=8)
            far_re[rows, :] = lre * scale
            far_im[rows, :] = lim * scale
    for t in range(64):
        here, there = slice(8 * t, 8 * t + 8), slice(504 - 8 * t, 512 - 8 * t)
        out_re[here, :] = re_ref[here, :] + far_re[there, :]
        out_im[here, :] = im_ref[here, :] - far_im[there, :]
    for a in range(8):
        tab = twist_ref[a]
        for i in range(5):
            cos_ref[a, i] = lane(tab, i)
            sin_ref[a, i] = lane(tab, 8 + i)


def middle_kernel(x_ref, twist_cos, twist_sin, filter_real, filter_imag, table_ref, out_ref,
                  re_ref, im_ref, re2_ref, im2_ref, tc_ref, ts_ref, fr_ref, fi_ref, sems):
    copies = [
        pltpu.make_async_copy(src, dst, sems.at[k])
        for k, (src, dst) in enumerate(
            [(twist_cos, tc_ref), (twist_sin, ts_ref), (filter_real, fr_ref), (filter_imag, fi_ref)]
        )
    ]
    for c in copies:
        c.start()
    copies[0].wait()
    copies[1].wait()

    def first(src):
        a = 8 * (src % 16) + src // 16
        scale = decode_scale(x_ref[src, 80:88, :])
        for i in range(5):
            x = decode_pair(x_ref[src, 16 * i : 16 * i + 16, :])
            put(re_ref, im_ref, i, a, times(x, scale * tc_ref[a, i], scale * ts_ref[a, i]))

    repeat(128, first, TD)

    def second(i):
        transform_128(re_ref, im_ref, i, -1)

    repeat(5, second)
    copies[2].wait()
    copies[3].wait()

    def third(at):
        b = at // 16 + 8 * (at % 16)
        x = []
        for j in range(8):
            across = pl.ds(at * 8 + j, 8, stride=STR)
            x.append((re_ref[across, :], im_ref[across, :]))
        for j in range(1, 8):
            x[j] = times(x[j], table_ref[16 * b + j], table_ref[16 * b + 8 + j])
        x = dft8(x, -1)
        y = []
        for e in range(8):
            rows = pl.ds(pl.multiple_of(8 * b, 8) + 1024 * e, 8)
            y.append(times(x[e], fr_ref[rows, :], fi_ref[rows, :]))
        y = dft8(y, 1)
        for j in range(8):
            if j:
                y[j] = times_conj(y[j], table_ref[16 * b + j], table_ref[16 * b + 8 + j])
            across = pl.ds(b * 8 + j, 8, stride=STR)
            re2_ref[across, :] = y[j][0]
            im2_ref[across, :] = y[j][1]

    repeat(128, third, TM)

    def fourth(i):
        transform_128(re2_ref, im2_ref, i, 1)

    repeat(5, fourth)

    def fifth(src):
        a = 8 * (src % 16) + src // 16
        blocks = []
        for i in range(5):
            blocks += times_conj(get(re2_ref, im2_ref, i, place(a)), tc_ref[a, i], ts_ref[a, i])

        def store(rows, v):
            out_ref[src, rows, :] = v

        encode(blocks, store)

    repeat(128, fifth, TE)


def backward_kernel(x_ref, table_ref, out_ref, re_ref, im_ref, conv_ref):
    def first(d):
        scale = decode_scale(x_ref[d, 80:88, :])
        for i in range(5):
            lre, lim = decode_pair(x_ref[d, 16 * i : 16 * i + 16, :])
            put(re_ref, im_ref, i, d, (lre * scale, lim * scale))

    repeat(128, first, TD)

    def second(i):
        transform_128(re_ref, im_ref, i, 1)

    repeat(5, second)

    def third(at):
        m = at // 16 + 8 * (at % 16)
        u0 = get(re_ref, im_ref, 0, at)[0]
        z = [times_conj(get(re_ref, im_ref, i, at), table_ref[16 * m + i], table_ref[16 * m + 8 + i]) for i in range(1, 4)]
        re4, im4 = get(re_ref, im_ref, 4, at)
        u4 = re4 * table_ref[16 * m + 4] + im4 * table_ref[16 * m + 12]
        (x1, y1), (x2, y2), (x3, y3) = z
        even, odd = u0 + u4, u0 - u4
        x13, y13 = x1 + x3, y1 - y3
        up, down = even + x2, even - x2
        conv_ref[0, m] = up + x13
        conv_ref[4, m] = up - x13
        conv_ref[2, m] = down - y13
        conv_ref[6, m] = down + y13
        aa, bb = (x1 - x3) * half_root, (y1 + y3) * half_root
        up, down = odd + y2, odd - y2
        diff, both = aa - bb, aa + bb
        conv_ref[1, m] = down + diff
        conv_ref[5, m] = down - diff
        conv_ref[3, m] = up - both
        conv_ref[7, m] = up + both

    repeat(128, third)

    def fourth(step):
        r, g = step // 8, step % 8
        blocks = [conv_ref[r, 16 * g + k] * (1.0 / 1048576.0) for k in range(16)]

        def store(rows, v):
            out_ref[r, g, rows, :] = v

        encode(blocks, store)

    repeat(64, fourth, TE)


def gate_kernel(x_ref, value_ref, gate_ref, skip_ref, out_ref):
    skip = skip_ref[0:1, :]

    def body(k):
        start = pl.multiple_of(16 * k, 16)
        for pair in range(4):
            sides = []
            for r in (2 * pair, 2 * pair + 1):
                scale = decode_scale(x_ref[r, 0, 128:136, :])
                low, high = decode_pair(x_ref[r, 0, pl.ds(start, 16), :])
                sides.append((low * scale, high * scale))
            for odd in range(2):
                conv = jnp.concatenate([sides[0][odd], sides[1][odd]], axis=0)
                rows = slice(16 * pair, 16 * pair + 16)
                v = value_ref[2 * k + odd, rows, :].astype(f32)
                g = gate_ref[2 * k + odd, rows, :].astype(f32)
                out_ref[2 * k + odd, rows, :] = (g * (conv + skip * v)).astype(bf16)

    repeat(8, body)


def roots_table(period):
    m, i = np.arange(128)[:, None], np.arange(8)[None, :]
    angle = -2.0 * np.pi * (m * i % period) / period
    return np.concatenate([np.cos(angle), np.sin(angle)], axis=1).astype(np.float32).reshape(-1)


def twist_table(device):
    shape = (128, 8, 128)
    lanes = lax.broadcasted_iota(jnp.int32, shape, 2)
    q = 8 * lax.broadcasted_iota(jnp.int32, shape, 0) + lax.broadcasted_iota(jnp.int32, shape, 1)
    kp = 8 * device + lanes % 8
    angle = (q * kp % 1048576).astype(f32) * (-2.0 * math.pi / 1048576.0)
    return jnp.where(lanes < 8, jnp.cos(angle), jnp.sin(angle))


twist_tables = twist_table


def vspec():
    return pl.BlockSpec(memory_space=pltpu.VMEM)


def sspec():
    return pl.BlockSpec(memory_space=pltpu.SMEM)


def aspec():
    return pl.BlockSpec(memory_space=pl.ANY)


def small_params():
    return params()


def params(mib=56):
    return pltpu.CompilerParams(vmem_limit_bytes=mib * 1024 * 1024)


def forward(columns, table):
    return pl.pallas_call(
        forward_kernel,
        out_shape=jax.ShapeDtypeStruct((128, 88, 128), bf16),
        in_specs=[vspec(), sspec()],
        out_specs=vspec(),
        scratch_shapes=[pltpu.VMEM((5 * STR, 128), f32)] * 2,
        compiler_params=params(16),
        name="forward_columns",
    )(columns, table)


def filter_codes(filter_real, filter_imag):
    rows = pl.BlockSpec((512, 128), lambda g: (g, 0))
    return pl.pallas_call(
        filter_kernel,
        grid=(16,),
        out_shape=jax.ShapeDtypeStruct((16, 3, 136, 128), bf16),
        in_specs=[rows, rows],
        out_specs=pl.BlockSpec((1, 3, 136, 128), lambda g: (g, 0, 0, 0)),
        compiler_params=small_params(),
        cost_estimate=pl.CostEstimate(flops=8000000, bytes_accessed=10 << 20, transcendentals=1000000),
        name="filter_codes",
    )(filter_real, filter_imag)


def prepare(filter_real, filter_imag, codes, twist):
    rows = pl.BlockSpec((512, 128), lambda g: (g, 0))
    wide = pl.BlockSpec((8, 5, 8, 128), lambda g: (g, 0, 0, 0))
    return pl.pallas_call(
        prepare_kernel,
        grid=(16,),
        out_shape=[jax.ShapeDtypeStruct((8192, 128), f32)] * 2 + [jax.ShapeDtypeStruct((128, 5, 8, 128), f32)] * 2,
        in_specs=[
            rows,
            rows,
            pl.BlockSpec((1, 3, 136, 128), lambda g: (15 - g, 0, 0, 0)),
            pl.BlockSpec((8, 8, 128), lambda g: (g, 0, 0)),
        ],
        out_specs=[rows, rows, wide, wide],
        scratch_shapes=[pltpu.VMEM((512, 128), f32)] * 2,
        compiler_params=small_params(),
        cost_estimate=pl.CostEstimate(flops=80000000000, bytes_accessed=25 << 20, transcendentals=1000000),
        name="prepare",
    )(filter_real, filter_imag, codes, twist)


def middle(arrived, twist_cos, twist_sin, filter_real, filter_imag, table):
    return pl.pallas_call(
        middle_kernel,
        out_shape=jax.ShapeDtypeStruct((128, 88, 128), bf16),
        in_specs=[vspec()] + [aspec()] * 4 + [sspec()],
        out_specs=vspec(),
        scratch_shapes=[pltpu.VMEM((8 * STR, 128), f32)] * 4
        + [pltpu.VMEM((128, 5, 8, 128), f32)] * 2
        + [pltpu.VMEM((8192, 128), f32)] * 2
        + [pltpu.SemaphoreType.DMA((4,))],
        compiler_params=params(44),
        name="filter_rows",
    )(arrived, twist_cos, twist_sin, filter_real, filter_imag, table)


def backward(returned, table):
    return pl.pallas_call(
        backward_kernel,
        out_shape=jax.ShapeDtypeStruct((8, 8, 136, 128), bf16),
        in_specs=[vspec(), sspec()],
        out_specs=vspec(),
        scratch_shapes=[pltpu.VMEM((5 * STR, 128), f32)] * 2 + [pltpu.VMEM((8, 128, 8, 128), f32)],
        compiler_params=params(24),
        name="backward_columns",
    )(returned, table)


def gating(settled, value, gate, skip):
    return pl.pallas_call(
        gate_kernel,
        grid=(8,),
        out_shape=jax.ShapeDtypeStruct((128, 64, 128), bf16),
        in_specs=[
            pl.BlockSpec((8, 1, 136, 128), lambda g: (0, g, 0, 0)),
            pl.BlockSpec((16, 64, 128), lambda g: (g, 0, 0)),
            pl.BlockSpec((16, 64, 128), lambda g: (g, 0, 0)),
            pl.BlockSpec((1, 128), lambda g: (0, 0)),
        ],
        out_specs=pl.BlockSpec((16, 64, 128), lambda g: (g, 0, 0)),
        compiler_params=params(16),
        name="gating",
    )(settled, value, gate, skip.reshape(1, 128))


def convolve(value, gate, filter_real, filter_imag, skip):
    device = lax.axis_index("row") * 16 + lax.axis_index("col")
    everyone = ("row", "col")
    table = jnp.asarray(roots_table(1024))
    filter_real = filter_real.reshape(8192, 128)
    filter_imag = filter_imag.reshape(8192, 128)
    pieces = value.reshape(128, 8, 8, 128)
    codes = filter_codes(filter_real, filter_imag)
    columns = lax.all_to_all(pieces, "row", split_axis=1, concat_axis=0, tiled=True)
    columns, codes = lax.optimization_barrier((columns, codes))
    codes = lax.ppermute(codes, everyone, [(d, 127 - d) for d in range(128)])
    spectrum = forward(columns.reshape(512, 16, 128), table)
    twist = twist_table(device)
    arrived = lax.all_to_all(spectrum, everyone, split_axis=0, concat_axis=0, tiled=True)
    both_real, both_imag, twist_cos, twist_sin = prepare(filter_real, filter_imag, codes, twist)
    leaving = middle(arrived, twist_cos, twist_sin, both_real, both_imag, table)
    returned = lax.all_to_all(leaving, everyone, split_axis=0, concat_axis=0, tiled=True)
    convolved = backward(returned, table)
    settled = lax.all_to_all(convolved, "row", split_axis=0, concat_axis=0, tiled=True)
    return gating(settled, value, gate, skip)


def solution(mesh):
    return jax.shard_map(
        convolve,
        mesh=mesh,
        in_specs=(
            P("row", "col", None),
            P("row", "col", None),
            P(None, ("row", "col"), None),
            P(None, ("row", "col"), None),
            P(),
        ),
        out_specs=P("row", "col", None),
        check_vma=False,
    )
```

```python
import math

import jax
import jax.numpy as jnp
import numpy as np
from jax import lax
from jax.experimental import pallas as pl
from jax.experimental.pallas import tpu as pltpu
from jax.sharding import PartitionSpec as P

GS = 2
TG = 4
TM = 1
TE = 16
TD = 16
half_root = math.sqrt(0.5)
span = 124.0
ln2 = math.log(2.0)
f32 = jnp.float32
bf16 = jnp.bfloat16


def turn(x, sign):
    re, im = x
    return (-im, re) if sign > 0 else (im, -re)


def add(x, y):
    return (x[0] + y[0], x[1] + y[1])


def sub(x, y):
    return (x[0] - y[0], x[1] - y[1])


def scale_root(x, index, period, sign):
    index %= period
    if index == 0:
        return x
    if 4 * index == period:
        return turn(x, sign)
    if 2 * index == period:
        return (-x[0], -x[1])
    re, im = x
    if 8 * index == period:
        if sign > 0:
            return ((re - im) * half_root, (im + re) * half_root)
        return ((re + im) * half_root, (im - re) * half_root)
    if 8 * index == 3 * period:
        if sign > 0:
            return ((re + im) * -half_root, (re - im) * half_root)
        return ((im - re) * half_root, (re + im) * -half_root)
    angle = 2.0 * math.pi * index / period
    c, s = math.cos(angle), sign * math.sin(angle)
    return (re * c - im * s, re * s + im * c)


def times(x, c, s):
    re, im = x
    return (re * c - im * s, re * s + im * c)


def times_conj(x, c, s):
    re, im = x
    return (re * c + im * s, im * c - re * s)


def dft4(y, sign):
    t0, t1 = add(y[0], y[2]), sub(y[0], y[2])
    t2, t3 = add(y[1], y[3]), turn(sub(y[1], y[3]), sign)
    return [add(t0, t2), add(t1, t3), sub(t0, t2), sub(t1, t3)]


def dft8(x, sign):
    even = dft4([add(x[k], x[k + 4]) for k in range(4)], sign)
    odd = dft4([scale_root(sub(x[k], x[k + 4]), k, 8, sign) for k in range(4)], sign)
    return [even[0], odd[0], even[1], odd[1], even[2], odd[2], even[3], odd[3]]


def dft16(x, sign):
    first = [dft4([x[4 * a + b] for a in range(4)], sign) for b in range(4)]
    out = [None] * 16
    for c in range(4):
        last = dft4([scale_root(first[b][c], b * c, 16, sign) for b in range(4)], sign)
        for e in range(4):
            out[c + 4 * e] = last[e]
    return out


STR = 1096


def rows_of(i, at):
    start = i * STR + at * 8
    if STR % 8 == 0 and not isinstance(start, int):
        start = pl.multiple_of(start, 8)
    return pl.ds(start, 8)


def get(re_ref, im_ref, i, at):
    rows = rows_of(i, at)
    return (re_ref[rows, :], im_ref[rows, :])


def put(re_ref, im_ref, i, at, x):
    rows = rows_of(i, at)
    re_ref[rows, :] = x[0]
    im_ref[rows, :] = x[1]


def transform_128(re_ref, im_ref, i, sign):
    for b in range(16):
        x = dft8([get(re_ref, im_ref, i, 17 * a + b) for a in range(8)], sign)
        for c in range(8):
            put(re_ref, im_ref, i, 17 * c + b, scale_root(x[c], b * c, 128, sign))
    for c in range(8):
        x = dft16([get(re_ref, im_ref, i, 17 * c + b) for b in range(16)], sign)
        for e in range(16):
            put(re_ref, im_ref, i, 17 * c + e, x[e])


def repeat(count, step, together=1):
    def body(k, carry):
        for u in range(together):
            step(together * k + u)
        return carry

    lax.fori_loop(0, count // together, body, 0)


def slot(n):
    return 17 * (n // 16) + n % 16


def place(k):
    return 17 * (k % 8) + k // 8


def encode(blocks, store):
    tops = [jnp.abs(x) for x in blocks]
    while len(tops) > 1:
        tops = [jnp.maximum(x, y) for x, y in zip(tops[::2], tops[1::2])] + tops[len(tops) // 2 * 2 :]
    scale = jnp.maximum(tops[0] * (1.0 / span), 1e-35).astype(bf16)
    inverse = 1.0 / scale.astype(f32)
    for k in range(len(blocks) // 2):
        pair = jnp.concatenate([blocks[2 * k] * inverse, blocks[2 * k + 1] * inverse], axis=0)
        store(slice(16 * k, 16 * k + 16), jnp.exp2(pair).astype(bf16))
    store(slice(8 * len(blocks), 8 * len(blocks) + 8), scale)


def decode_scale(rows):
    return rows.astype(f32) * (1.0 / ln2)


def decode_pair(rows):
    logs = jnp.log(rows.astype(f32))
    return logs[0:8], logs[8:16]


def forward_kernel(x_ref, table_ref, out_ref, re_ref, im_ref):
    def first(pair):
        both = [x_ref[64 * r + pair].astype(f32) for r in range(8)]
        for odd in range(2):
            m = 2 * pair + odd
            at = slot(m)
            x = [v[8 * odd : 8 * odd + 8] for v in both]
            s = [x[k] + x[k + 4] for k in range(4)]
            d = [x[k] - x[k + 4] for k in range(4)]
            s02, s13 = s[0] + s[2], s[1] + s[3]
            put(re_ref, im_ref, 0, at, (s02 + s13, jnp.zeros_like(s02)))
            low, high = (d[1] - d[3]) * half_root, (d[1] + d[3]) * half_root
            rows = [None, (d[0] + low, -d[2] - high), (s[0] - s[2], s[3] - s[1]), (d[0] - low, d[2] - high)]
            for i in range(1, 4):
                put(re_ref, im_ref, i, at, times(rows[i], table_ref[16 * m + i], table_ref[16 * m + 8 + i]))
            mid = s02 - s13
            put(re_ref, im_ref, 4, at, (mid * table_ref[16 * m + 4], mid * table_ref[16 * m + 12]))

    repeat(64, first)

    def second(i):
        transform_128(re_ref, im_ref, i, -1)

    repeat(5, second)

    def third(d):
        blocks = []
        for i in range(5):
            blocks += get(re_ref, im_ref, i, place(d))

        def store(rows, v):
            out_ref[d, rows, :] = v

        encode(blocks, store)

    repeat(128, third, TE)


def lane(x, k):
    return jnp.broadcast_to(x[:, k : k + 1], (8, 128))


def filter_kernel(re_ref, im_ref, out_ref):
    for s in range(3):
        blocks = []
        for u in range(8):
            rows = pl.ds(64 * u + 7 - s, 8, stride=8)
            blocks += [re_ref[rows, :], im_ref[rows, :]]

        def store(rows, v):
            out_ref[0, s, rows, :] = v

        encode(blocks, store)


def twist_kernel(twist_ref, cos_ref, sin_ref):
    for a in range(32):
        tab = twist_ref[a]
        for i in range(5):
            cos_ref[a, i] = lane(tab, i)
            sin_ref[a, i] = lane(tab, 8 + i)


def merge_kernel(re_ref, im_ref, code_ref, out_re, out_im, far_re, far_im):
    far_re[...] = jnp.zeros((1024, 128), f32)
    far_im[...] = jnp.zeros((1024, 128), f32)
    for g in range(2):
        for s in range(3):
            scale = decode_scale(code_ref[g, s, 128:136, :])
            for u in range(8):
                lre, lim = decode_pair(code_ref[g, s, 16 * u : 16 * u + 16, :])
                rows = pl.ds(512 * g + 64 * u + s + 1, 8, stride=8)
                far_re[rows, :] = lre * scale
                far_im[rows, :] = lim * scale
    for t in range(128):
        here, there = slice(8 * t, 8 * t + 8), slice(1016 - 8 * t, 1024 - 8 * t)
        out_re[here, :] = re_ref[here, :] + far_re[there, :]
        out_im[here, :] = im_ref[here, :] - far_im[there, :]


def middle_kernel(x_ref, twist_cos, twist_sin, filter_real, filter_imag, root_ref, out_ref,
                  re_ref, im_ref, re2_ref, im2_ref, tc_ref, ts_ref, fr_ref, fi_ref, sems):
    parts = []
    for k in range(4):
        rows = pl.ds(32 * k, 32)
        parts.append(
            [
                pltpu.make_async_copy(twist_cos.at[rows], tc_ref.at[rows], sems.at[2 * k]),
                pltpu.make_async_copy(twist_sin.at[rows], ts_ref.at[rows], sems.at[2 * k + 1]),
            ]
        )
    parts.append(
        [
            pltpu.make_async_copy(filter_real, fr_ref, sems.at[8]),
            pltpu.make_async_copy(filter_imag, fi_ref, sems.at[9]),
        ]
    )
    for part in parts:
        for c in part:
            c.start()

    def first(src):
        a = 8 * (src % 16) + src // 16
        scale = decode_scale(x_ref[src, 80:88, :])
        for i in range(5):
            x = decode_pair(x_ref[src, 16 * i : 16 * i + 16, :])
            put(re_ref, im_ref, i, slot(a), times(x, scale * tc_ref[src, i], scale * ts_ref[src, i]))

    for k in range(4):
        for c in parts[k]:
            c.wait()
        repeat(32, lambda src, k=k: first(32 * k + src), TD)

    def second(i):
        transform_128(re_ref, im_ref, i, -1)

    repeat(5, second)
    for c in parts[4]:
        c.wait()

    def third(e):
        start = 136 * (e // 2) + 64 * (e % 2)
        for i in range(5):
            x = []
            for j in range(8):
                rows = pl.ds(i * STR + 8 * e + j, 8, stride=136)
                x.append((re_ref[rows, :], im_ref[rows, :]))
            for j in range(1, 8):
                x[j] = times(x[j], root_ref[0, e, j], root_ref[1, e, j])
            x = dft8(x, -1)
            y = []
            for k in range(8):
                rows = pl.ds(64 * e + 1024 * k + i, 8, stride=8)
                y.append(times(x[k], fr_ref[rows, :], fi_ref[rows, :]))
            y = dft8(y, 1)
            for j in range(8):
                if j:
                    y[j] = times_conj(y[j], root_ref[0, e, j], root_ref[1, e, j])
                rows = pl.ds(i * STR + start + j, 8, stride=8)
                re2_ref[rows, :] = y[j][0]
                im2_ref[rows, :] = y[j][1]

    repeat(16, third, TM)

    def fourth(i):
        transform_128(re2_ref, im2_ref, i, 1)

    repeat(5, fourth)

    def fifth(src):
        a = 8 * (src % 16) + src // 16
        blocks = []
        for i in range(5):
            blocks += times_conj(get(re2_ref, im2_ref, i, place(a)), tc_ref[src, i], ts_ref[src, i])

        def store(rows, v):
            out_ref[src, rows, :] = v

        encode(blocks, store)

    repeat(128, fifth, TE)


def backward_kernel(x_ref, table_ref, out_ref, re_ref, im_ref, conv_ref):
    def first(d):
        scale = decode_scale(x_ref[d, 80:88, :])
        for i in range(5):
            lre, lim = decode_pair(x_ref[d, 16 * i : 16 * i + 16, :])
            put(re_ref, im_ref, i, slot(d), (lre * scale, lim * scale))

    repeat(128, first, TD)

    def second(i):
        transform_128(re_ref, im_ref, i, 1)

    repeat(5, second)

    def third(m):
        at = place(m)
        u0 = get(re_ref, im_ref, 0, at)[0]
        z = [times_conj(get(re_ref, im_ref, i, at), table_ref[16 * m + i], table_ref[16 * m + 8 + i]) for i in range(1, 4)]
        re4, im4 = get(re_ref, im_ref, 4, at)
        u4 = re4 * table_ref[16 * m + 4] + im4 * table_ref[16 * m + 12]
        (x1, y1), (x2, y2), (x3, y3) = z
        even, odd = u0 + u4, u0 - u4
        x13, y13 = x1 + x3, y1 - y3
        up, down = even + x2, even - x2
        conv_ref[0, m] = up + x13
        conv_ref[4, m] = up - x13
        conv_ref[2, m] = down - y13
        conv_ref[6, m] = down + y13
        aa, bb = (x1 - x3) * half_root, (y1 + y3) * half_root
        up, down = odd + y2, odd - y2
        diff, both = aa - bb, aa + bb
        conv_ref[1, m] = down + diff
        conv_ref[5, m] = down - diff
        conv_ref[3, m] = up - both
        conv_ref[7, m] = up + both

    repeat(128, third)

    def fourth(step):
        r, g = step // 8, step % 8
        blocks = [conv_ref[r, 16 * g + k] * (1.0 / 1048576.0) for k in range(16)]

        def store(rows, v):
            out_ref[r, g, rows, :] = v

        encode(blocks, store)

    repeat(64, fourth, TE)


def gate_kernel(x_ref, value_ref, gate_ref, skip_ref, out_ref):
    skip = skip_ref[0:1, :]

    def body(at):
        g, k = at // 8, at % 8
        start = pl.multiple_of(16 * k, 16)
        for pair in range(4):
            sides = []
            for r in (2 * pair, 2 * pair + 1):
                scale = decode_scale(x_ref[r, g, 128:136, :])
                low, high = decode_pair(x_ref[r, g, pl.ds(start, 16), :])
                sides.append((low * scale, high * scale))
            for odd in range(2):
                conv = jnp.concatenate([sides[0][odd], sides[1][odd]], axis=0)
                rows = slice(16 * pair, 16 * pair + 16)
                v = value_ref[2 * at + odd, rows, :].astype(f32)
                w = gate_ref[2 * at + odd, rows, :].astype(f32)
                out_ref[2 * at + odd, rows, :] = (w * (conv + skip * v)).astype(bf16)

    repeat(64 // GS, body, TG)


def roots_table(period):
    m, i = np.arange(128)[:, None], np.arange(8)[None, :]
    angle = -2.0 * np.pi * (m * i % period) / period
    return np.concatenate([np.cos(angle), np.sin(angle)], axis=1).astype(np.float32).reshape(-1)


def wide_roots():
    e, j, c = np.arange(16)[:, None, None], np.arange(8)[None, :, None], np.arange(8)[None, None, :]
    angle = -2.0 * np.pi * (j * (c + 8 * e) % 1024) / 1024
    both = np.stack([np.cos(angle), np.sin(angle)]).astype(np.float32)
    return np.broadcast_to(both[..., None], (2, 16, 8, 8, 128))


def twist_table(device):
    shape = (128, 8, 128)
    lanes = lax.broadcasted_iota(jnp.int32, shape, 2)
    source = lax.broadcasted_iota(jnp.int32, shape, 0)
    q = 64 * (source % 16) + 8 * (source // 16) + lax.broadcasted_iota(jnp.int32, shape, 1)
    kp = 8 * device + lanes % 8
    angle = (q * kp % 1048576).astype(f32) * (-2.0 * math.pi / 1048576.0)
    return jnp.where(lanes < 8, jnp.cos(angle), jnp.sin(angle))


twist_tables = twist_table


def vspec():
    return pl.BlockSpec(memory_space=pltpu.VMEM)


def sspec():
    return pl.BlockSpec(memory_space=pltpu.SMEM)


def aspec():
    return pl.BlockSpec(memory_space=pl.ANY)


def small_params():
    return params()


def params(mib=56):
    return pltpu.CompilerParams(vmem_limit_bytes=mib * 1024 * 1024)


def forward(columns, table):
    return pl.pallas_call(
        forward_kernel,
        out_shape=jax.ShapeDtypeStruct((128, 88, 128), bf16),
        in_specs=[vspec(), sspec()],
        out_specs=vspec(),
        scratch_shapes=[pltpu.VMEM((5 * STR, 128), f32)] * 2,
        compiler_params=params(16),
        name="forward_columns",
    )(columns, table)


def filter_codes(filter_real, filter_imag):
    rows = pl.BlockSpec((512, 128), lambda g: (g, 0))
    return pl.pallas_call(
        filter_kernel,
        grid=(16,),
        out_shape=jax.ShapeDtypeStruct((16, 3, 136, 128), bf16),
        in_specs=[rows, rows],
        out_specs=pl.BlockSpec((1, 3, 136, 128), lambda g: (g, 0, 0, 0)),
        compiler_params=small_params(),
        cost_estimate=pl.CostEstimate(flops=8000000, bytes_accessed=10 << 20, transcendentals=1000000),
        name="filter_codes",
    )(filter_real, filter_imag)


def twists(twist):
    wide = pl.BlockSpec((32, 5, 8, 128), lambda g: (g, 0, 0, 0))
    return pl.pallas_call(
        twist_kernel,
        grid=(4,),
        out_shape=[jax.ShapeDtypeStruct((128, 5, 8, 128), f32)] * 2,
        in_specs=[pl.BlockSpec((32, 8, 128), lambda g: (g, 0, 0))],
        out_specs=[wide, wide],
        compiler_params=small_params(),
        cost_estimate=pl.CostEstimate(flops=8000000, bytes_accessed=6 << 20, transcendentals=0),
        name="twists",
    )(twist)


def merged(filter_real, filter_imag, codes):
    rows = pl.BlockSpec((1024, 128), lambda g: (g, 0))
    return pl.pallas_call(
        merge_kernel,
        grid=(8,),
        out_shape=[jax.ShapeDtypeStruct((8192, 128), f32)] * 2,
        in_specs=[rows, rows, pl.BlockSpec((2, 3, 136, 128), lambda g: (7 - g, 0, 0, 0))],
        out_specs=[rows, rows],
        scratch_shapes=[pltpu.VMEM((1024, 128), f32)] * 2,
        compiler_params=small_params(),
        cost_estimate=pl.CostEstimate(flops=80000000000, bytes_accessed=18 << 20, transcendentals=0),
        name="merge_filters",
    )(filter_real, filter_imag, codes)


def middle(arrived, twist_cos, twist_sin, filter_real, filter_imag, table):
    return pl.pallas_call(
        middle_kernel,
        out_shape=jax.ShapeDtypeStruct((128, 88, 128), bf16),
        in_specs=[vspec()] + [aspec()] * 4 + [vspec()],
        out_specs=vspec(),
        scratch_shapes=[pltpu.VMEM((8 * STR, 128), f32)] * 4
        + [pltpu.VMEM((128, 5, 8, 128), f32)] * 2
        + [pltpu.VMEM((8192, 128), f32)] * 2
        + [pltpu.SemaphoreType.DMA((10,))],
        compiler_params=params(50),
        name="filter_rows",
    )(arrived, twist_cos, twist_sin, filter_real, filter_imag, table)


def backward(returned, table):
    return pl.pallas_call(
        backward_kernel,
        out_shape=jax.ShapeDtypeStruct((8, 8, 136, 128), bf16),
        in_specs=[vspec(), sspec()],
        out_specs=vspec(),
        scratch_shapes=[pltpu.VMEM((5 * STR, 128), f32)] * 2 + [pltpu.VMEM((8, 128, 8, 128), f32)],
        compiler_params=params(24),
        name="backward_columns",
    )(returned, table)


def gating(settled, value, gate, skip):
    return pl.pallas_call(
        gate_kernel,
        grid=(GS,),
        out_shape=jax.ShapeDtypeStruct((128, 64, 128), bf16),
        in_specs=[
            pl.BlockSpec((8, 8 // GS, 136, 128), lambda g: (0, g, 0, 0)),
            pl.BlockSpec((128 // GS, 64, 128), lambda g: (g, 0, 0)),
            pl.BlockSpec((128 // GS, 64, 128), lambda g: (g, 0, 0)),
            pl.BlockSpec((1, 128), lambda g: (0, 0)),
        ],
        out_specs=pl.BlockSpec((128 // GS, 64, 128), lambda g: (g, 0, 0)),
        compiler_params=params(16),
        name="gating",
    )(settled, value, gate, skip.reshape(1, 128))


def convolve(value, gate, filter_real, filter_imag, skip):
    device = lax.axis_index("row") * 16 + lax.axis_index("col")
    everyone = ("row", "col")
    table = jnp.asarray(roots_table(1024))
    filter_real = filter_real.reshape(8192, 128)
    filter_imag = filter_imag.reshape(8192, 128)
    pieces = value.reshape(128, 8, 8, 128)
    codes = filter_codes(filter_real, filter_imag)
    columns = lax.all_to_all(pieces, "row", split_axis=1, concat_axis=0, tiled=True)
    columns, codes = lax.optimization_barrier((columns, codes))
    codes = lax.ppermute(codes, everyone, [(d, 127 - d) for d in range(128)])
    spectrum = forward(columns.reshape(512, 16, 128), table)
    spectrum, device = lax.optimization_barrier((spectrum, device))
    twist = twist_table(device)
    arrived = lax.all_to_all(spectrum, everyone, split_axis=0, concat_axis=0, tiled=True)
    twist_cos, twist_sin = twists(twist)
    both_real, both_imag = merged(filter_real, filter_imag, codes)
    leaving = middle(arrived, twist_cos, twist_sin, both_real, both_imag, jnp.asarray(wide_roots()))
    returned = lax.all_to_all(leaving, everyone, split_axis=0, concat_axis=0, tiled=True)
    convolved = backward(returned, table)
    settled = lax.all_to_all(convolved, "row", split_axis=0, concat_axis=0, tiled=True)
    return gating(settled, value, gate, skip)


def solution(mesh):
    return jax.shard_map(
        convolve,
        mesh=mesh,
        in_specs=(
            P("row", "col", None),
            P("row", "col", None),
            P(None, ("row", "col"), None),
            P(None, ("row", "col"), None),
            P(),
        ),
        out_specs=P("row", "col", None),
        check_vma=False,
    )
```

```python
import math

import jax
import jax.numpy as jnp
import numpy as np
from jax import lax
from jax.experimental import pallas as pl
from jax.experimental.pallas import tpu as pltpu
from jax.sharding import PartitionSpec as P

GS = 2
TG = 4
TM = 1
TE = 16
TD = 16
half_root = math.sqrt(0.5)
span = 124.0
ln2 = math.log(2.0)
f32 = jnp.float32
bf16 = jnp.bfloat16


def turn(x, sign):
    re, im = x
    return (-im, re) if sign > 0 else (im, -re)


def add(x, y):
    return (x[0] + y[0], x[1] + y[1])


def sub(x, y):
    return (x[0] - y[0], x[1] - y[1])


def scale_root(x, index, period, sign):
    index %= period
    if index == 0:
        return x
    if 4 * index == period:
        return turn(x, sign)
    if 2 * index == period:
        return (-x[0], -x[1])
    re, im = x
    if 8 * index == period:
        if sign > 0:
            return ((re - im) * half_root, (im + re) * half_root)
        return ((re + im) * half_root, (im - re) * half_root)
    if 8 * index == 3 * period:
        if sign > 0:
            return ((re + im) * -half_root, (re - im) * half_root)
        return ((im - re) * half_root, (re + im) * -half_root)
    angle = 2.0 * math.pi * index / period
    c, s = math.cos(angle), sign * math.sin(angle)
    return (re * c - im * s, re * s + im * c)


def times(x, c, s):
    re, im = x
    return (re * c - im * s, re * s + im * c)


def times_conj(x, c, s):
    re, im = x
    return (re * c + im * s, im * c - re * s)


def dft4(y, sign):
    t0, t1 = add(y[0], y[2]), sub(y[0], y[2])
    t2, t3 = add(y[1], y[3]), turn(sub(y[1], y[3]), sign)
    return [add(t0, t2), add(t1, t3), sub(t0, t2), sub(t1, t3)]


def dft8(x, sign):
    even = dft4([add(x[k], x[k + 4]) for k in range(4)], sign)
    odd = dft4([scale_root(sub(x[k], x[k + 4]), k, 8, sign) for k in range(4)], sign)
    return [even[0], odd[0], even[1], odd[1], even[2], odd[2], even[3], odd[3]]


def dft16(x, sign):
    first = [dft4([x[4 * a + b] for a in range(4)], sign) for b in range(4)]
    out = [None] * 16
    for c in range(4):
        last = dft4([scale_root(first[b][c], b * c, 16, sign) for b in range(4)], sign)
        for e in range(4):
            out[c + 4 * e] = last[e]
    return out


STR = 1096


def rows_of(i, at):
    start = i * STR + at * 8
    if STR % 8 == 0 and not isinstance(start, int):
        start = pl.multiple_of(start, 8)
    return pl.ds(start, 8)


def get(re_ref, im_ref, i, at):
    rows = rows_of(i, at)
    return (re_ref[rows, :], im_ref[rows, :])


def put(re_ref, im_ref, i, at, x):
    rows = rows_of(i, at)
    re_ref[rows, :] = x[0]
    im_ref[rows, :] = x[1]


def transform_128(re_ref, im_ref, i, sign):
    for b in range(16):
        x = dft8([get(re_ref, im_ref, i, 17 * a + b) for a in range(8)], sign)
        for c in range(8):
            put(re_ref, im_ref, i, 17 * c + b, scale_root(x[c], b * c, 128, sign))
    for c in range(8):
        x = dft16([get(re_ref, im_ref, i, 17 * c + b) for b in range(16)], sign)
        for e in range(16):
            put(re_ref, im_ref, i, 17 * c + e, x[e])


def repeat(count, step, together=1):
    def body(k, carry):
        for u in range(together):
            step(together * k + u)
        return carry

    lax.fori_loop(0, count // together, body, 0)


def slot(n):
    return 17 * (n // 16) + n % 16


def place(k):
    return 17 * (k % 8) + k // 8


def encode(blocks, store):
    tops = [jnp.abs(x) for x in blocks]
    while len(tops) > 1:
        tops = [jnp.maximum(x, y) for x, y in zip(tops[::2], tops[1::2])] + tops[len(tops) // 2 * 2 :]
    scale = jnp.maximum(tops[0] * (1.0 / span), 1e-35).astype(bf16)
    inverse = 1.0 / scale.astype(f32)
    for k in range(len(blocks) // 2):
        pair = jnp.concatenate([blocks[2 * k] * inverse, blocks[2 * k + 1] * inverse], axis=0)
        store(slice(16 * k, 16 * k + 16), jnp.exp2(pair).astype(bf16))
    store(slice(8 * len(blocks), 8 * len(blocks) + 8), scale)


def decode_scale(rows):
    return rows.astype(f32) * (1.0 / ln2)


def decode_pair(rows):
    logs = jnp.log(rows.astype(f32))
    return logs[0:8], logs[8:16]


def forward_kernel(x_ref, table_ref, out_ref, re_ref, im_ref):
    def first(pair):
        both = [x_ref[64 * r + pair].astype(f32) for r in range(8)]
        for odd in range(2):
            m = 2 * pair + odd
            at = slot(m)
            x = [v[8 * odd : 8 * odd + 8] for v in both]
            s = [x[k] + x[k + 4] for k in range(4)]
            d = [x[k] - x[k + 4] for k in range(4)]
            s02, s13 = s[0] + s[2], s[1] + s[3]
            put(re_ref, im_ref, 0, at, (s02 + s13, jnp.zeros_like(s02)))
            low, high = (d[1] - d[3]) * half_root, (d[1] + d[3]) * half_root
            rows = [None, (d[0] + low, -d[2] - high), (s[0] - s[2], s[3] - s[1]), (d[0] - low, d[2] - high)]
            for i in range(1, 4):
                put(re_ref, im_ref, i, at, times(rows[i], table_ref[16 * m + i], table_ref[16 * m + 8 + i]))
            mid = s02 - s13
            put(re_ref, im_ref, 4, at, (mid * table_ref[16 * m + 4], mid * table_ref[16 * m + 12]))

    repeat(64, first)

    def second(i):
        transform_128(re_ref, im_ref, i, -1)

    repeat(5, second)

    def third(d):
        blocks = []
        for i in range(5):
            blocks += get(re_ref, im_ref, i, place(d))

        def store(rows, v):
            out_ref[d, rows, :] = v

        encode(blocks, store)

    repeat(128, third, TE)


def filter_kernel(re_ref, im_ref, out_ref):
    for s in range(3):
        blocks = []
        for u in range(8):
            rows = pl.ds(64 * u + 7 - s, 8, stride=8)
            blocks += [re_ref[rows, :], im_ref[rows, :]]

        def store(rows, v):
            out_ref[0, s, rows, :] = v

        encode(blocks, store)


def merge_kernel(re_ref, im_ref, code_ref, out_re, out_im, far_re, far_im):
    far_re[...] = jnp.zeros((1024, 128), f32)
    far_im[...] = jnp.zeros((1024, 128), f32)
    for g in range(2):
        for s in range(3):
            scale = decode_scale(code_ref[g, s, 128:136, :])
            for u in range(8):
                lre, lim = decode_pair(code_ref[g, s, 16 * u : 16 * u + 16, :])
                rows = pl.ds(512 * g + 64 * u + s + 1, 8, stride=8)
                far_re[rows, :] = lre * scale
                far_im[rows, :] = lim * scale
    for t in range(128):
        here, there = slice(8 * t, 8 * t + 8), slice(1016 - 8 * t, 1024 - 8 * t)
        out_re[here, :] = re_ref[here, :] + far_re[there, :]
        out_im[here, :] = im_ref[here, :] - far_im[there, :]


def middle_kernel(x_ref, far_ref, near_ref, filter_real, filter_imag, root_ref, out_ref,
                  re_ref, im_ref, re2_ref, im2_ref, tc_ref, ts_ref, fr_ref, fi_ref, sems):
    copies = [
        pltpu.make_async_copy(filter_real, fr_ref, sems.at[0]),
        pltpu.make_async_copy(filter_imag, fi_ref, sems.at[1]),
    ]
    for c in copies:
        c.start()

    def first(src):
        a = 8 * (src % 16) + src // 16
        scale = decode_scale(x_ref[src, 80:88, :])
        for i in range(5):
            x = decode_pair(x_ref[src, 16 * i : 16 * i + 16, :])
            c, s = times((near_ref[0, i], near_ref[1, i]), far_ref[16 * src + i], far_ref[16 * src + 8 + i])
            tc_ref[src, i] = c
            ts_ref[src, i] = s
            put(re_ref, im_ref, i, slot(a), times(x, scale * c, scale * s))

    repeat(128, first, TD)

    def second(i):
        transform_128(re_ref, im_ref, i, -1)

    repeat(5, second)
    for c in copies:
        c.wait()

    def third(e):
        start = 136 * (e // 2) + 64 * (e % 2)
        for i in range(5):
            x = []
            for j in range(8):
                rows = pl.ds(i * STR + 8 * e + j, 8, stride=136)
                x.append((re_ref[rows, :], im_ref[rows, :]))
            for j in range(1, 8):
                x[j] = times(x[j], root_ref[0, e, j], root_ref[1, e, j])
            x = dft8(x, -1)
            y = []
            for k in range(8):
                rows = pl.ds(64 * e + 1024 * k + i, 8, stride=8)
                y.append(times(x[k], fr_ref[rows, :], fi_ref[rows, :]))
            y = dft8(y, 1)
            for j in range(8):
                if j:
                    y[j] = times_conj(y[j], root_ref[0, e, j], root_ref[1, e, j])
                rows = pl.ds(i * STR + start + j, 8, stride=8)
                re2_ref[rows, :] = y[j][0]
                im2_ref[rows, :] = y[j][1]

    repeat(16, third, TM)

    def fourth(i):
        transform_128(re2_ref, im2_ref, i, 1)

    repeat(5, fourth)

    def fifth(src):
        a = 8 * (src % 16) + src // 16
        blocks = []
        for i in range(5):
            blocks += times_conj(get(re2_ref, im2_ref, i, place(a)), tc_ref[src, i], ts_ref[src, i])

        def store(rows, v):
            out_ref[src, rows, :] = v

        encode(blocks, store)

    repeat(128, fifth, TE)


def backward_kernel(x_ref, table_ref, out_ref, re_ref, im_ref, conv_ref):
    def first(d):
        scale = decode_scale(x_ref[d, 80:88, :])
        for i in range(5):
            lre, lim = decode_pair(x_ref[d, 16 * i : 16 * i + 16, :])
            put(re_ref, im_ref, i, slot(d), (lre * scale, lim * scale))

    repeat(128, first, TD)

    def second(i):
        transform_128(re_ref, im_ref, i, 1)

    repeat(5, second)

    def third(m):
        at = place(m)
        u0 = get(re_ref, im_ref, 0, at)[0]
        z = [times_conj(get(re_ref, im_ref, i, at), table_ref[16 * m + i], table_ref[16 * m + 8 + i]) for i in range(1, 4)]
        re4, im4 = get(re_ref, im_ref, 4, at)
        u4 = re4 * table_ref[16 * m + 4] + im4 * table_ref[16 * m + 12]
        (x1, y1), (x2, y2), (x3, y3) = z
        even, odd = u0 + u4, u0 - u4
        x13, y13 = x1 + x3, y1 - y3
        up, down = even + x2, even - x2
        conv_ref[0, m] = up + x13
        conv_ref[4, m] = up - x13
        conv_ref[2, m] = down - y13
        conv_ref[6, m] = down + y13
        aa, bb = (x1 - x3) * half_root, (y1 + y3) * half_root
        up, down = odd + y2, odd - y2
        diff, both = aa - bb, aa + bb
        conv_ref[1, m] = down + diff
        conv_ref[5, m] = down - diff
        conv_ref[3, m] = up - both
        conv_ref[7, m] = up + both

    repeat(128, third)

    def fourth(step):
        r, g = step // 8, step % 8
        blocks = [conv_ref[r, 16 * g + k] * (1.0 / 1048576.0) for k in range(16)]

        def store(rows, v):
            out_ref[r, g, rows, :] = v

        encode(blocks, store)

    repeat(64, fourth, TE)


def gate_kernel(x_ref, value_ref, gate_ref, skip_ref, out_ref):
    skip = skip_ref[0:1, :]

    def body(at):
        g, k = at // 8, at % 8
        start = pl.multiple_of(16 * k, 16)
        for pair in range(4):
            sides = []
            for r in (2 * pair, 2 * pair + 1):
                scale = decode_scale(x_ref[r, g, 128:136, :])
                low, high = decode_pair(x_ref[r, g, pl.ds(start, 16), :])
                sides.append((low * scale, high * scale))
            for odd in range(2):
                conv = jnp.concatenate([sides[0][odd], sides[1][odd]], axis=0)
                rows = slice(16 * pair, 16 * pair + 16)
                v = value_ref[2 * at + odd, rows, :].astype(f32)
                w = gate_ref[2 * at + odd, rows, :].astype(f32)
                out_ref[2 * at + odd, rows, :] = (w * (conv + skip * v)).astype(bf16)

    repeat(64 // GS, body, TG)


def roots_table(period):
    m, i = np.arange(128)[:, None], np.arange(8)[None, :]
    angle = -2.0 * np.pi * (m * i % period) / period
    return np.concatenate([np.cos(angle), np.sin(angle)], axis=1).astype(np.float32).reshape(-1)


def wide_roots():
    e, j, c = np.arange(16)[:, None, None], np.arange(8)[None, :, None], np.arange(8)[None, None, :]
    angle = -2.0 * np.pi * (j * (c + 8 * e) % 1024) / 1024
    both = np.stack([np.cos(angle), np.sin(angle)]).astype(np.float32)
    return np.broadcast_to(both[..., None], (2, 16, 8, 8, 128))


def twist_tables(device):
    unit = -2.0 * math.pi / 1048576.0
    source = lax.broadcasted_iota(jnp.int32, (128, 16), 0)
    i = lax.broadcasted_iota(jnp.int32, (128, 16), 1)
    angle = ((64 * (source % 16) + 8 * (source // 16)) * (8 * device + i % 8) % 1048576).astype(f32) * unit
    far = jnp.where(i < 8, jnp.cos(angle), jnp.sin(angle)).reshape(-1)
    shape = (8, 8, 128)
    kp = 8 * device + lax.broadcasted_iota(jnp.int32, shape, 0)
    angle = (kp * lax.broadcasted_iota(jnp.int32, shape, 1)).astype(f32) * unit
    return far, jnp.stack([jnp.cos(angle), jnp.sin(angle)])


def vspec():
    return pl.BlockSpec(memory_space=pltpu.VMEM)


def sspec():
    return pl.BlockSpec(memory_space=pltpu.SMEM)


def aspec():
    return pl.BlockSpec(memory_space=pl.ANY)


def params(mib=56):
    return pltpu.CompilerParams(vmem_limit_bytes=mib * 1024 * 1024)


def forward(columns, table):
    return pl.pallas_call(
        forward_kernel,
        out_shape=jax.ShapeDtypeStruct((128, 88, 128), bf16),
        in_specs=[vspec(), sspec()],
        out_specs=vspec(),
        scratch_shapes=[pltpu.VMEM((5 * STR, 128), f32)] * 2,
        compiler_params=params(16),
        name="forward_columns",
    )(columns, table)


def filter_codes(filter_real, filter_imag):
    rows = pl.BlockSpec((512, 128), lambda g: (g, 0))
    return pl.pallas_call(
        filter_kernel,
        grid=(16,),
        out_shape=jax.ShapeDtypeStruct((16, 3, 136, 128), bf16),
        in_specs=[rows, rows],
        out_specs=pl.BlockSpec((1, 3, 136, 128), lambda g: (g, 0, 0, 0)),
        compiler_params=params(),
        cost_estimate=pl.CostEstimate(flops=8000000, bytes_accessed=10 << 20, transcendentals=1000000),
        name="filter_codes",
    )(filter_real, filter_imag)


def merged(filter_real, filter_imag, codes):
    rows = pl.BlockSpec((1024, 128), lambda g: (g, 0))
    return pl.pallas_call(
        merge_kernel,
        grid=(8,),
        out_shape=[jax.ShapeDtypeStruct((8192, 128), f32)] * 2,
        in_specs=[rows, rows, pl.BlockSpec((2, 3, 136, 128), lambda g: (7 - g, 0, 0, 0))],
        out_specs=[rows, rows],
        scratch_shapes=[pltpu.VMEM((1024, 128), f32)] * 2,
        compiler_params=params(),
        cost_estimate=pl.CostEstimate(flops=80000000000, bytes_accessed=18 << 20, transcendentals=0),
        name="merge_filters",
    )(filter_real, filter_imag, codes)


def middle(arrived, far, near, filter_real, filter_imag, roots):
    return pl.pallas_call(
        middle_kernel,
        out_shape=jax.ShapeDtypeStruct((128, 88, 128), bf16),
        in_specs=[vspec(), sspec(), vspec(), aspec(), aspec(), vspec()],
        out_specs=vspec(),
        scratch_shapes=[pltpu.VMEM((5 * STR, 128), f32)] * 4
        + [pltpu.VMEM((128, 5, 8, 128), f32)] * 2
        + [pltpu.VMEM((8192, 128), f32)] * 2
        + [pltpu.SemaphoreType.DMA((2,))],
        compiler_params=params(50),
        name="filter_rows",
    )(arrived, far, near, filter_real, filter_imag, roots)


def backward(returned, table):
    return pl.pallas_call(
        backward_kernel,
        out_shape=jax.ShapeDtypeStruct((8, 8, 136, 128), bf16),
        in_specs=[vspec(), sspec()],
        out_specs=vspec(),
        scratch_shapes=[pltpu.VMEM((5 * STR, 128), f32)] * 2 + [pltpu.VMEM((8, 128, 8, 128), f32)],
        compiler_params=params(24),
        name="backward_columns",
    )(returned, table)


def gating(settled, value, gate, skip):
    return pl.pallas_call(
        gate_kernel,
        grid=(GS,),
        out_shape=jax.ShapeDtypeStruct((128, 64, 128), bf16),
        in_specs=[
            pl.BlockSpec((8, 8 // GS, 136, 128), lambda g: (0, g, 0, 0)),
            pl.BlockSpec((128 // GS, 64, 128), lambda g: (g, 0, 0)),
            pl.BlockSpec((128 // GS, 64, 128), lambda g: (g, 0, 0)),
            pl.BlockSpec((1, 128), lambda g: (0, 0)),
        ],
        out_specs=pl.BlockSpec((128 // GS, 64, 128), lambda g: (g, 0, 0)),
        compiler_params=params(16),
        name="gating",
    )(settled, value, gate, skip.reshape(1, 128))


def convolve(value, gate, filter_real, filter_imag, skip):
    device = lax.axis_index("row") * 16 + lax.axis_index("col")
    everyone = ("row", "col")
    table = jnp.asarray(roots_table(1024))
    filter_real = filter_real.reshape(8192, 128)
    filter_imag = filter_imag.reshape(8192, 128)
    pieces = value.reshape(128, 8, 8, 128)
    codes = filter_codes(filter_real, filter_imag)
    columns = lax.all_to_all(pieces, "row", split_axis=1, concat_axis=0, tiled=True)
    columns, codes = lax.optimization_barrier((columns, codes))
    codes = lax.ppermute(codes, everyone, [(d, 127 - d) for d in range(128)])
    spectrum = forward(columns.reshape(512, 16, 128), table)
    spectrum, device = lax.optimization_barrier((spectrum, device))
    far, near = twist_tables(device)
    arrived = lax.all_to_all(spectrum, everyone, split_axis=0, concat_axis=0, tiled=True)
    both_real, both_imag = merged(filter_real, filter_imag, codes)
    leaving = middle(arrived, far, near, both_real, both_imag, jnp.asarray(wide_roots()))
    returned = lax.all_to_all(leaving, everyone, split_axis=0, concat_axis=0, tiled=True)
    convolved = backward(returned, table)
    settled = lax.all_to_all(convolved, "row", split_axis=0, concat_axis=0, tiled=True)
    return gating(settled, value, gate, skip)


def solution(mesh):
    return jax.shard_map(
        convolve,
        mesh=mesh,
        in_specs=(
            P("row", "col", None),
            P("row", "col", None),
            P(None, ("row", "col"), None),
            P(None, ("row", "col"), None),
            P(),
        ),
        out_specs=P("row", "col", None),
        check_vma=False,
    )
```

```python
import math

import jax
import jax.numpy as jnp
import numpy as np
from jax import lax
from jax.experimental import pallas as pl
from jax.experimental.pallas import tpu as pltpu
from jax.sharding import PartitionSpec as P

GS = 2
TG = 4
LV = 56
TM = 1
TE = 16
TD = 16
half_root = math.sqrt(0.5)
span = 124.0
ln2 = math.log(2.0)
f32 = jnp.float32
bf16 = jnp.bfloat16


def turn(x, sign):
    re, im = x
    return (-im, re) if sign > 0 else (im, -re)


def add(x, y):
    return (x[0] + y[0], x[1] + y[1])


def sub(x, y):
    return (x[0] - y[0], x[1] - y[1])


def scale_root(x, index, period, sign):
    index %= period
    if index == 0:
        return x
    if 4 * index == period:
        return turn(x, sign)
    if 2 * index == period:
        return (-x[0], -x[1])
    re, im = x
    if 8 * index == period:
        if sign > 0:
            return ((re - im) * half_root, (im + re) * half_root)
        return ((re + im) * half_root, (im - re) * half_root)
    if 8 * index == 3 * period:
        if sign > 0:
            return ((re + im) * -half_root, (re - im) * half_root)
        return ((im - re) * half_root, (re + im) * -half_root)
    angle = 2.0 * math.pi * index / period
    c, s = math.cos(angle), sign * math.sin(angle)
    return (re * c - im * s, re * s + im * c)


def times(x, c, s):
    re, im = x
    return (re * c - im * s, re * s + im * c)


def times_conj(x, c, s):
    re, im = x
    return (re * c + im * s, im * c - re * s)


def dft4(y, sign):
    t0, t1 = add(y[0], y[2]), sub(y[0], y[2])
    t2, t3 = add(y[1], y[3]), turn(sub(y[1], y[3]), sign)
    return [add(t0, t2), add(t1, t3), sub(t0, t2), sub(t1, t3)]


def dft8(x, sign):
    even = dft4([add(x[k], x[k + 4]) for k in range(4)], sign)
    odd = dft4([scale_root(sub(x[k], x[k + 4]), k, 8, sign) for k in range(4)], sign)
    return [even[0], odd[0], even[1], odd[1], even[2], odd[2], even[3], odd[3]]


def dft16(x, sign):
    first = [dft4([x[4 * a + b] for a in range(4)], sign) for b in range(4)]
    out = [None] * 16
    for c in range(4):
        last = dft4([scale_root(first[b][c], b * c, 16, sign) for b in range(4)], sign)
        for e in range(4):
            out[c + 4 * e] = last[e]
    return out


STR = 1096


def rows_of(i, at):
    start = i * STR + at * 8
    if STR % 8 == 0 and not isinstance(start, int):
        start = pl.multiple_of(start, 8)
    return pl.ds(start, 8)


def get(re_ref, im_ref, i, at):
    rows = rows_of(i, at)
    return (re_ref[rows, :], im_ref[rows, :])


def put(re_ref, im_ref, i, at, x):
    rows = rows_of(i, at)
    re_ref[rows, :] = x[0]
    im_ref[rows, :] = x[1]


def transform_128(re_ref, im_ref, i, sign):
    for b in range(16):
        x = dft8([get(re_ref, im_ref, i, 17 * a + b) for a in range(8)], sign)
        for c in range(8):
            put(re_ref, im_ref, i, 17 * c + b, scale_root(x[c], b * c, 128, sign))
    for c in range(8):
        x = dft16([get(re_ref, im_ref, i, 17 * c + b) for b in range(16)], sign)
        for e in range(16):
            put(re_ref, im_ref, i, 17 * c + e, x[e])


def repeat(count, step, together=1):
    def body(k, carry):
        for u in range(together):
            step(together * k + u)
        return carry

    lax.fori_loop(0, count // together, body, 0)


def slot(n):
    return 17 * (n // 16) + n % 16


def place(k):
    return 17 * (k % 8) + k // 8


def encode(blocks, store):
    tops = [jnp.abs(x) for x in blocks]
    while len(tops) > 1:
        tops = [jnp.maximum(x, y) for x, y in zip(tops[::2], tops[1::2])] + tops[len(tops) // 2 * 2 :]
    scale = jnp.maximum(tops[0] * (1.0 / span), 1e-35).astype(bf16)
    inverse = 1.0 / scale.astype(f32)
    for k in range(len(blocks) // 2):
        pair = jnp.concatenate([blocks[2 * k] * inverse, blocks[2 * k + 1] * inverse], axis=0)
        store(slice(16 * k, 16 * k + 16), jnp.exp2(pair).astype(bf16))
    store(slice(8 * len(blocks), 8 * len(blocks) + 8), scale)


def decode_scale(rows):
    return rows.astype(f32) * (1.0 / ln2)


def decode_pair(rows):
    logs = jnp.log(rows.astype(f32))
    return logs[0:8], logs[8:16]


def forward_kernel(x_ref, table_ref, out_ref, re_ref, im_ref):
    def first(pair):
        both = [x_ref[64 * r + pair].astype(f32) for r in range(8)]
        for odd in range(2):
            m = 2 * pair + odd
            at = slot(m)
            x = [v[8 * odd : 8 * odd + 8] for v in both]
            s = [x[k] + x[k + 4] for k in range(4)]
            d = [x[k] - x[k + 4] for k in range(4)]
            s02, s13 = s[0] + s[2], s[1] + s[3]
            put(re_ref, im_ref, 0, at, (s02 + s13, jnp.zeros_like(s02)))
            low, high = (d[1] - d[3]) * half_root, (d[1] + d[3]) * half_root
            rows = [None, (d[0] + low, -d[2] - high), (s[0] - s[2], s[3] - s[1]), (d[0] - low, d[2] - high)]
            for i in range(1, 4):
                put(re_ref, im_ref, i, at, times(rows[i], table_ref[16 * m + i], table_ref[16 * m + 8 + i]))
            mid = s02 - s13
            put(re_ref, im_ref, 4, at, (mid * table_ref[16 * m + 4], mid * table_ref[16 * m + 12]))

    repeat(64, first)

    def second(i):
        transform_128(re_ref, im_ref, i, -1)

    repeat(5, second)

    def third(d):
        blocks = []
        for i in range(5):
            blocks += get(re_ref, im_ref, i, place(d))

        def store(rows, v):
            out_ref[d, rows, :] = v

        encode(blocks, store)

    repeat(128, third, TE)


def leave_kernel(value_hbm, real_hbm, imag_hbm, out_ref, code_ref, value_ref, re_ref, im_ref, sems):
    copies = [pltpu.make_async_copy(value_hbm, value_ref, sems.at[0])]
    for g in range(8):
        rows = pl.ds(1024 * g, 1024)
        copies.append(pltpu.make_async_copy(real_hbm.at[rows], re_ref.at[rows], sems.at[1 + g]))
        copies.append(pltpu.make_async_copy(imag_hbm.at[rows], im_ref.at[rows], sems.at[9 + g]))
    for c in copies:
        c.start()
    copies[0].wait()

    def first(k):
        for pair in range(4):
            rows = slice(16 * pair, 16 * pair + 16)
            low, high = value_ref[2 * k, rows, :].astype(f32), value_ref[2 * k + 1, rows, :].astype(f32)
            for odd in range(2):
                half = slice(8 * odd, 8 * odd + 8)
                out_ref[2 * pair + odd, k] = jnp.concatenate([low[half], high[half]], axis=0).astype(bf16)

    repeat(64, first, 8)
    for g in range(8):
        copies[1 + 2 * g].wait()
        copies[2 + 2 * g].wait()
        for s in range(3):
            blocks = []
            for u in range(16):
                rows = pl.ds(1024 * g + 64 * u + 7 - s, 8, stride=8)
                blocks += [re_ref[rows, :], im_ref[rows, :]]

            def store(rows, v, g=g, s=s):
                code_ref[g, s, rows, :] = v

            encode(blocks, store)


def merge_kernel(re_ref, im_ref, code_ref, out_re, out_im, far_re, far_im):
    far_re[...] = jnp.zeros((1024, 128), f32)
    far_im[...] = jnp.zeros((1024, 128), f32)
    for s in range(3):
        scale = decode_scale(code_ref[0, s, 256:264, :])
        for u in range(16):
            lre, lim = decode_pair(code_ref[0, s, 16 * u : 16 * u + 16, :])
            rows = pl.ds(64 * u + s + 1, 8, stride=8)
            far_re[rows, :] = lre * scale
            far_im[rows, :] = lim * scale
    for t in range(128):
        here, there = slice(8 * t, 8 * t + 8), slice(1016 - 8 * t, 1024 - 8 * t)
        out_re[here, :] = re_ref[here, :] + far_re[there, :]
        out_im[here, :] = im_ref[here, :] - far_im[there, :]


def middle_kernel(x_ref, far_ref, near_ref, filter_real, filter_imag, root_ref, out_ref,
                  re_ref, im_ref, re2_ref, im2_ref, tc_ref, ts_ref, fr_ref, fi_ref, sems):
    copies = [
        pltpu.make_async_copy(filter_real, fr_ref, sems.at[0]),
        pltpu.make_async_copy(filter_imag, fi_ref, sems.at[1]),
    ]
    for c in copies:
        c.start()

    def first(src):
        a = 8 * (src % 16) + src // 16
        scale = decode_scale(x_ref[src, 80:88, :])
        for i in range(5):
            x = decode_pair(x_ref[src, 16 * i : 16 * i + 16, :])
            c, s = times((near_ref[0, i], near_ref[1, i]), far_ref[16 * src + i], far_ref[16 * src + 8 + i])
            tc_ref[src, i] = c
            ts_ref[src, i] = s
            put(re_ref, im_ref, i, slot(a), times(x, scale * c, scale * s))

    repeat(128, first, TD)

    def second(i):
        transform_128(re_ref, im_ref, i, -1)

    repeat(5, second)
    for c in copies:
        c.wait()

    def third(e):
        start = 136 * (e // 2) + 64 * (e % 2)
        for i in range(5):
            x = []
            for j in range(8):
                rows = pl.ds(i * STR + 8 * e + j, 8, stride=136)
                x.append((re_ref[rows, :], im_ref[rows, :]))
            for j in range(1, 8):
                x[j] = times(x[j], root_ref[0, e, j], root_ref[1, e, j])
            x = dft8(x, -1)
            y = []
            for k in range(8):
                rows = pl.ds(64 * e + 1024 * k + i, 8, stride=8)
                y.append(times(x[k], fr_ref[rows, :], fi_ref[rows, :]))
            y = dft8(y, 1)
            for j in range(8):
                if j:
                    y[j] = times_conj(y[j], root_ref[0, e, j], root_ref[1, e, j])
                rows = pl.ds(i * STR + start + j, 8, stride=8)
                re2_ref[rows, :] = y[j][0]
                im2_ref[rows, :] = y[j][1]

    repeat(16, third, TM)

    def fourth(i):
        transform_128(re2_ref, im2_ref, i, 1)

    repeat(5, fourth)

    def fifth(src):
        a = 8 * (src % 16) + src // 16
        blocks = []
        for i in range(5):
            blocks += times_conj(get(re2_ref, im2_ref, i, place(a)), tc_ref[src, i], ts_ref[src, i])

        def store(rows, v):
            out_ref[src, rows, :] = v

        encode(blocks, store)

    repeat(128, fifth, TE)


def backward_kernel(x_ref, table_ref, out_ref, re_ref, im_ref, conv_ref):
    def first(d):
        scale = decode_scale(x_ref[d, 80:88, :])
        for i in range(5):
            lre, lim = decode_pair(x_ref[d, 16 * i : 16 * i + 16, :])
            put(re_ref, im_ref, i, slot(d), (lre * scale, lim * scale))

    repeat(128, first, TD)

    def second(i):
        transform_128(re_ref, im_ref, i, 1)

    repeat(5, second)

    def third(m):
        at = place(m)
        u0 = get(re_ref, im_ref, 0, at)[0]
        z = [times_conj(get(re_ref, im_ref, i, at), table_ref[16 * m + i], table_ref[16 * m + 8 + i]) for i in range(1, 4)]
        re4, im4 = get(re_ref, im_ref, 4, at)
        u4 = re4 * table_ref[16 * m + 4] + im4 * table_ref[16 * m + 12]
        (x1, y1), (x2, y2), (x3, y3) = z
        even, odd = u0 + u4, u0 - u4
        x13, y13 = x1 + x3, y1 - y3
        up, down = even + x2, even - x2
        conv_ref[0, m] = up + x13
        conv_ref[4, m] = up - x13
        conv_ref[2, m] = down - y13
        conv_ref[6, m] = down + y13
        aa, bb = (x1 - x3) * half_root, (y1 + y3) * half_root
        up, down = odd + y2, odd - y2
        diff, both = aa - bb, aa + bb
        conv_ref[1, m] = down + diff
        conv_ref[5, m] = down - diff
        conv_ref[3, m] = up - both
        conv_ref[7, m] = up + both

    repeat(128, third)

    def fourth(step):
        r, g = step // 4, step % 4
        blocks = [conv_ref[r, 32 * g + k] * (1.0 / 1048576.0) for k in range(32)]

        def store(rows, v):
            out_ref[r, g, rows, :] = v

        encode(blocks, store)

    repeat(32, fourth, 8)


def gate_kernel(x_ref, value_ref, gate_ref, skip_ref, out_ref):
    skip = skip_ref[0:1, :]

    def body(at):
        g, k = at // 16, at % 16
        start = pl.multiple_of(16 * k, 16)
        for pair in range(4):
            sides = []
            for r in (2 * pair, 2 * pair + 1):
                scale = decode_scale(x_ref[r, g, 256:264, :])
                low, high = decode_pair(x_ref[r, g, pl.ds(start, 16), :])
                sides.append((low * scale, high * scale))
            for odd in range(2):
                conv = jnp.concatenate([sides[0][odd], sides[1][odd]], axis=0)
                rows = slice(16 * pair, 16 * pair + 16)
                v = value_ref[2 * at + odd, rows, :].astype(f32)
                w = gate_ref[2 * at + odd, rows, :].astype(f32)
                out_ref[2 * at + odd, rows, :] = (w * (conv + skip * v)).astype(bf16)

    repeat(64 // GS, body, TG)


def roots_table(period):
    m, i = np.arange(128)[:, None], np.arange(8)[None, :]
    angle = -2.0 * np.pi * (m * i % period) / period
    return np.concatenate([np.cos(angle), np.sin(angle)], axis=1).astype(np.float32).reshape(-1)


def wide_roots():
    e, j, c = np.arange(16)[:, None, None], np.arange(8)[None, :, None], np.arange(8)[None, None, :]
    angle = -2.0 * np.pi * (j * (c + 8 * e) % 1024) / 1024
    both = np.stack([np.cos(angle), np.sin(angle)]).astype(np.float32)
    return np.broadcast_to(both[..., None], (2, 16, 8, 8, 128))


def twist_tables(device):
    unit = -2.0 * math.pi / 1048576.0
    source = lax.broadcasted_iota(jnp.int32, (128, 16), 0)
    i = lax.broadcasted_iota(jnp.int32, (128, 16), 1)
    angle = ((64 * (source % 16) + 8 * (source // 16)) * (8 * device + i % 8) % 1048576).astype(f32) * unit
    far = jnp.where(i < 8, jnp.cos(angle), jnp.sin(angle)).reshape(-1)
    shape = (8, 8, 128)
    kp = 8 * device + lax.broadcasted_iota(jnp.int32, shape, 0)
    angle = (kp * lax.broadcasted_iota(jnp.int32, shape, 1)).astype(f32) * unit
    return far, jnp.stack([jnp.cos(angle), jnp.sin(angle)])


def vspec():
    return pl.BlockSpec(memory_space=pltpu.VMEM)


def sspec():
    return pl.BlockSpec(memory_space=pltpu.SMEM)


def aspec():
    return pl.BlockSpec(memory_space=pl.ANY)


def params(mib=56):
    return pltpu.CompilerParams(vmem_limit_bytes=mib * 1024 * 1024)


def forward(columns, table):
    return pl.pallas_call(
        forward_kernel,
        out_shape=jax.ShapeDtypeStruct((128, 88, 128), bf16),
        in_specs=[vspec(), sspec()],
        out_specs=vspec(),
        scratch_shapes=[pltpu.VMEM((5 * STR, 128), f32)] * 2,
        compiler_params=params(16),
        name="forward_columns",
    )(columns, table)


def leave(value, filter_real, filter_imag):
    return pl.pallas_call(
        leave_kernel,
        out_shape=[jax.ShapeDtypeStruct((8, 64, 16, 128), bf16), jax.ShapeDtypeStruct((8, 3, 264, 128), bf16)],
        in_specs=[aspec()] * 3,
        out_specs=[vspec()] * 2,
        scratch_shapes=[pltpu.VMEM((128, 64, 128), bf16)]
        + [pltpu.VMEM((8192, 128), f32)] * 2
        + [pltpu.SemaphoreType.DMA((17,))],
        compiler_params=params(LV),
        cost_estimate=pl.CostEstimate(flops=8000000, bytes_accessed=14 << 20, transcendentals=1000000),
        name="leave",
    )(value, filter_real, filter_imag)


def merged(filter_real, filter_imag, codes):
    rows = pl.BlockSpec((1024, 128), lambda g: (g, 0))
    return pl.pallas_call(
        merge_kernel,
        grid=(8,),
        out_shape=[jax.ShapeDtypeStruct((8192, 128), f32)] * 2,
        in_specs=[rows, rows, pl.BlockSpec((1, 3, 264, 128), lambda g: (7 - g, 0, 0, 0))],
        out_specs=[rows, rows],
        scratch_shapes=[pltpu.VMEM((1024, 128), f32)] * 2,
        compiler_params=params(),
        cost_estimate=pl.CostEstimate(flops=80000000000, bytes_accessed=18 << 20, transcendentals=0),
        name="merge_filters",
    )(filter_real, filter_imag, codes)


def middle(arrived, far, near, filter_real, filter_imag, roots):
    return pl.pallas_call(
        middle_kernel,
        out_shape=jax.ShapeDtypeStruct((128, 88, 128), bf16),
        in_specs=[vspec(), sspec(), vspec(), aspec(), aspec(), vspec()],
        out_specs=vspec(),
        scratch_shapes=[pltpu.VMEM((5 * STR, 128), f32)] * 4
        + [pltpu.VMEM((128, 5, 8, 128), f32)] * 2
        + [pltpu.VMEM((8192, 128), f32)] * 2
        + [pltpu.SemaphoreType.DMA((2,))],
        compiler_params=params(50),
        name="filter_rows",
    )(arrived, far, near, filter_real, filter_imag, roots)


def backward(returned, table):
    return pl.pallas_call(
        backward_kernel,
        out_shape=jax.ShapeDtypeStruct((8, 4, 264, 128), bf16),
        in_specs=[vspec(), sspec()],
        out_specs=vspec(),
        scratch_shapes=[pltpu.VMEM((5 * STR, 128), f32)] * 2 + [pltpu.VMEM((8, 128, 8, 128), f32)],
        compiler_params=params(24),
        name="backward_columns",
    )(returned, table)


def gating(settled, value, gate, skip):
    return pl.pallas_call(
        gate_kernel,
        grid=(GS,),
        out_shape=jax.ShapeDtypeStruct((128, 64, 128), bf16),
        in_specs=[
            pl.BlockSpec((8, 4 // GS, 264, 128), lambda g: (0, g, 0, 0)),
            pl.BlockSpec((128 // GS, 64, 128), lambda g: (g, 0, 0)),
            pl.BlockSpec((128 // GS, 64, 128), lambda g: (g, 0, 0)),
            pl.BlockSpec((1, 128), lambda g: (0, 0)),
        ],
        out_specs=pl.BlockSpec((128 // GS, 64, 128), lambda g: (g, 0, 0)),
        compiler_params=params(16),
        name="gating",
    )(settled, value, gate, skip.reshape(1, 128))


def convolve(value, gate, filter_real, filter_imag, skip):
    device = lax.axis_index("row") * 16 + lax.axis_index("col")
    everyone = ("row", "col")
    table = jnp.asarray(roots_table(1024))
    filter_real = filter_real.reshape(8192, 128)
    filter_imag = filter_imag.reshape(8192, 128)
    pieces, codes = leave(value, filter_real, filter_imag)
    columns = lax.all_to_all(pieces, "row", split_axis=0, concat_axis=0, tiled=True)
    columns, codes = lax.optimization_barrier((columns, codes))
    codes = lax.ppermute(codes, everyone, [(d, 127 - d) for d in range(128)])
    spectrum = forward(columns.reshape(512, 16, 128), table)
    spectrum, device = lax.optimization_barrier((spectrum, device))
    far, near = twist_tables(device)
    arrived = lax.all_to_all(spectrum, everyone, split_axis=0, concat_axis=0, tiled=True)
    both_real, both_imag = merged(filter_real, filter_imag, codes)
    leaving = middle(arrived, far, near, both_real, both_imag, jnp.asarray(wide_roots()))
    returned = lax.all_to_all(leaving, everyone, split_axis=0, concat_axis=0, tiled=True)
    convolved = backward(returned, table)
    settled = lax.all_to_all(convolved, "row", split_axis=0, concat_axis=0, tiled=True)
    return gating(settled, value, gate, skip)


def solution(mesh):
    return jax.shard_map(
        convolve,
        mesh=mesh,
        in_specs=(
            P("row", "col", None),
            P("row", "col", None),
            P(None, ("row", "col"), None),
            P(None, ("row", "col"), None),
            P(),
        ),
        out_specs=P("row", "col", None),
        check_vma=False,
    )
```

```python
import math

import jax
import jax.numpy as jnp
import numpy as np
from jax import lax
from jax.experimental import pallas as pl
from jax.experimental.pallas import tpu as pltpu
from jax.sharding import PartitionSpec as P

GS = 2
TG = 4
LV = 56
TM = 1
TE = 16
TD = 16
half_root = math.sqrt(0.5)
span = 124.0
ln2 = math.log(2.0)
f32 = jnp.float32
bf16 = jnp.bfloat16


def turn(x, sign):
    re, im = x
    return (-im, re) if sign > 0 else (im, -re)


def add(x, y):
    return (x[0] + y[0], x[1] + y[1])


def sub(x, y):
    return (x[0] - y[0], x[1] - y[1])


def scale_root(x, index, period, sign):
    index %= period
    if index == 0:
        return x
    if 4 * index == period:
        return turn(x, sign)
    if 2 * index == period:
        return (-x[0], -x[1])
    re, im = x
    if 8 * index == period:
        if sign > 0:
            return ((re - im) * half_root, (im + re) * half_root)
        return ((re + im) * half_root, (im - re) * half_root)
    if 8 * index == 3 * period:
        if sign > 0:
            return ((re + im) * -half_root, (re - im) * half_root)
        return ((im - re) * half_root, (re + im) * -half_root)
    angle = 2.0 * math.pi * index / period
    c, s = math.cos(angle), sign * math.sin(angle)
    return (re * c - im * s, re * s + im * c)


def times(x, c, s):
    re, im = x
    return (re * c - im * s, re * s + im * c)


def times_conj(x, c, s):
    re, im = x
    return (re * c + im * s, im * c - re * s)


def dft4(y, sign):
    t0, t1 = add(y[0], y[2]), sub(y[0], y[2])
    t2, t3 = add(y[1], y[3]), turn(sub(y[1], y[3]), sign)
    return [add(t0, t2), add(t1, t3), sub(t0, t2), sub(t1, t3)]


def dft8(x, sign):
    even = dft4([add(x[k], x[k + 4]) for k in range(4)], sign)
    odd = dft4([scale_root(sub(x[k], x[k + 4]), k, 8, sign) for k in range(4)], sign)
    return [even[0], odd[0], even[1], odd[1], even[2], odd[2], even[3], odd[3]]


def dft16(x, sign):
    first = [dft4([x[4 * a + b] for a in range(4)], sign) for b in range(4)]
    out = [None] * 16
    for c in range(4):
        last = dft4([scale_root(first[b][c], b * c, 16, sign) for b in range(4)], sign)
        for e in range(4):
            out[c + 4 * e] = last[e]
    return out


STR = 1096


def rows_of(i, at):
    start = i * STR + at * 8
    if STR % 8 == 0 and not isinstance(start, int):
        start = pl.multiple_of(start, 8)
    return pl.ds(start, 8)


def get(re_ref, im_ref, i, at):
    rows = rows_of(i, at)
    return (re_ref[rows, :], im_ref[rows, :])


def put(re_ref, im_ref, i, at, x):
    rows = rows_of(i, at)
    re_ref[rows, :] = x[0]
    im_ref[rows, :] = x[1]


def transform_128(re_ref, im_ref, i, sign):
    for b in range(16):
        x = dft8([get(re_ref, im_ref, i, 17 * a + b) for a in range(8)], sign)
        for c in range(8):
            put(re_ref, im_ref, i, 17 * c + b, scale_root(x[c], b * c, 128, sign))
    for c in range(8):
        x = dft16([get(re_ref, im_ref, i, 17 * c + b) for b in range(16)], sign)
        for e in range(16):
            put(re_ref, im_ref, i, 17 * c + e, x[e])


def repeat(count, step, together=1):
    def body(k, carry):
        for u in range(together):
            step(together * k + u)
        return carry

    lax.fori_loop(0, count // together, body, 0)


def slot(n):
    return 17 * (n // 16) + n % 16


def place(k):
    return 17 * (k % 8) + k // 8


def send_parts(step, count, together, src_ref, dst_ref, sems):
    size = src_ref.shape[0] // 4

    def copy(k):
        rows = pl.ds(size * k, size)
        return pltpu.make_async_copy(src_ref.at[rows], dst_ref.at[rows], sems.at[k])

    def part(k, carry):
        repeat(count // 4, lambda n: step(count // 4 * k + n), together)
        copy(k).start()
        return carry

    lax.fori_loop(0, 4, part, 0)
    for k in range(4):
        copy(k).wait()


def encode(blocks, store):
    tops = [jnp.abs(x) for x in blocks]
    while len(tops) > 1:
        tops = [jnp.maximum(x, y) for x, y in zip(tops[::2], tops[1::2])] + tops[len(tops) // 2 * 2 :]
    scale = jnp.maximum(tops[0] * (1.0 / span), 1e-35).astype(bf16)
    inverse = 1.0 / scale.astype(f32)
    for k in range(len(blocks) // 2):
        pair = jnp.concatenate([blocks[2 * k] * inverse, blocks[2 * k + 1] * inverse], axis=0)
        store(slice(16 * k, 16 * k + 16), jnp.exp2(pair).astype(bf16))
    store(slice(8 * len(blocks), 8 * len(blocks) + 8), scale)


def decode_scale(rows):
    return rows.astype(f32) * (1.0 / ln2)


def decode_pair(rows):
    logs = jnp.log(rows.astype(f32))
    return logs[0:8], logs[8:16]


def forward_kernel(x_ref, table_ref, out_hbm, re_ref, im_ref, out_ref, sems):
    def first(pair):
        both = [x_ref[64 * r + pair].astype(f32) for r in range(8)]
        for odd in range(2):
            m = 2 * pair + odd
            at = slot(m)
            x = [v[8 * odd : 8 * odd + 8] for v in both]
            s = [x[k] + x[k + 4] for k in range(4)]
            d = [x[k] - x[k + 4] for k in range(4)]
            s02, s13 = s[0] + s[2], s[1] + s[3]
            put(re_ref, im_ref, 0, at, (s02 + s13, jnp.zeros_like(s02)))
            low, high = (d[1] - d[3]) * half_root, (d[1] + d[3]) * half_root
            rows = [None, (d[0] + low, -d[2] - high), (s[0] - s[2], s[3] - s[1]), (d[0] - low, d[2] - high)]
            for i in range(1, 4):
                put(re_ref, im_ref, i, at, times(rows[i], table_ref[16 * m + i], table_ref[16 * m + 8 + i]))
            mid = s02 - s13
            put(re_ref, im_ref, 4, at, (mid * table_ref[16 * m + 4], mid * table_ref[16 * m + 12]))

    repeat(64, first)

    def second(i):
        transform_128(re_ref, im_ref, i, -1)

    repeat(5, second)

    def third(d):
        blocks = []
        for i in range(5):
            blocks += get(re_ref, im_ref, i, place(d))

        def store(rows, v):
            out_ref[d, rows, :] = v

        encode(blocks, store)

    send_parts(third, 128, TE, out_ref, out_hbm, sems)


def leave_kernel(value_hbm, real_hbm, imag_hbm, out_ref, code_ref, value_ref, re_ref, im_ref, sems):
    copies = [pltpu.make_async_copy(value_hbm, value_ref, sems.at[0])]
    for g in range(8):
        rows = pl.ds(1024 * g, 1024)
        copies.append(pltpu.make_async_copy(real_hbm.at[rows], re_ref.at[rows], sems.at[1 + g]))
        copies.append(pltpu.make_async_copy(imag_hbm.at[rows], im_ref.at[rows], sems.at[9 + g]))
    for c in copies:
        c.start()
    copies[0].wait()

    def first(k):
        for pair in range(4):
            rows = slice(16 * pair, 16 * pair + 16)
            low, high = value_ref[2 * k, rows, :].astype(f32), value_ref[2 * k + 1, rows, :].astype(f32)
            for odd in range(2):
                half = slice(8 * odd, 8 * odd + 8)
                out_ref[2 * pair + odd, k] = jnp.concatenate([low[half], high[half]], axis=0).astype(bf16)

    repeat(64, first, 8)
    for g in range(8):
        copies[1 + 2 * g].wait()
        copies[2 + 2 * g].wait()
        for s in range(3):
            blocks = []
            for u in range(16):
                rows = pl.ds(1024 * g + 64 * u + 7 - s, 8, stride=8)
                blocks += [re_ref[rows, :], im_ref[rows, :]]

            def store(rows, v, g=g, s=s):
                code_ref[g, s, rows, :] = v

            encode(blocks, store)


def merge_kernel(re_ref, im_ref, code_ref, out_re, out_im, far_re, far_im):
    far_re[...] = jnp.zeros((1024, 128), f32)
    far_im[...] = jnp.zeros((1024, 128), f32)
    for s in range(3):
        scale = decode_scale(code_ref[0, s, 256:264, :])
        for u in range(16):
            lre, lim = decode_pair(code_ref[0, s, 16 * u : 16 * u + 16, :])
            rows = pl.ds(64 * u + s + 1, 8, stride=8)
            far_re[rows, :] = lre * scale
            far_im[rows, :] = lim * scale
    for t in range(128):
        here, there = slice(8 * t, 8 * t + 8), slice(1016 - 8 * t, 1024 - 8 * t)
        out_re[here, :] = re_ref[here, :] + far_re[there, :]
        out_im[here, :] = im_ref[here, :] - far_im[there, :]


def middle_kernel(x_ref, far_ref, near_ref, filter_real, filter_imag, root_ref, out_hbm,
                  re_ref, im_ref, re2_ref, im2_ref, tc_ref, ts_ref, fr_ref, fi_ref, out_ref, sems, out_sems):
    copies = [
        pltpu.make_async_copy(filter_real, fr_ref, sems.at[0]),
        pltpu.make_async_copy(filter_imag, fi_ref, sems.at[1]),
    ]
    for c in copies:
        c.start()

    def first(src):
        a = 8 * (src % 16) + src // 16
        scale = decode_scale(x_ref[src, 80:88, :])
        for i in range(5):
            x = decode_pair(x_ref[src, 16 * i : 16 * i + 16, :])
            c, s = times((near_ref[0, i], near_ref[1, i]), far_ref[16 * src + i], far_ref[16 * src + 8 + i])
            tc_ref[src, i] = c
            ts_ref[src, i] = s
            put(re_ref, im_ref, i, slot(a), times(x, scale * c, scale * s))

    repeat(128, first, TD)

    def second(i):
        transform_128(re_ref, im_ref, i, -1)

    repeat(5, second)
    for c in copies:
        c.wait()

    def third(e):
        start = 136 * (e // 2) + 64 * (e % 2)
        for i in range(5):
            x = []
            for j in range(8):
                rows = pl.ds(i * STR + 8 * e + j, 8, stride=136)
                x.append((re_ref[rows, :], im_ref[rows, :]))
            for j in range(1, 8):
                x[j] = times(x[j], root_ref[0, e, j], root_ref[1, e, j])
            x = dft8(x, -1)
            y = []
            for k in range(8):
                rows = pl.ds(64 * e + 1024 * k + i, 8, stride=8)
                y.append(times(x[k], fr_ref[rows, :], fi_ref[rows, :]))
            y = dft8(y, 1)
            for j in range(8):
                if j:
                    y[j] = times_conj(y[j], root_ref[0, e, j], root_ref[1, e, j])
                rows = pl.ds(i * STR + start + j, 8, stride=8)
                re2_ref[rows, :] = y[j][0]
                im2_ref[rows, :] = y[j][1]

    repeat(16, third, TM)

    def fourth(i):
        transform_128(re2_ref, im2_ref, i, 1)

    repeat(5, fourth)

    def fifth(src):
        a = 8 * (src % 16) + src // 16
        blocks = []
        for i in range(5):
            blocks += times_conj(get(re2_ref, im2_ref, i, place(a)), tc_ref[src, i], ts_ref[src, i])

        def store(rows, v):
            out_ref[src, rows, :] = v

        encode(blocks, store)

    send_parts(fifth, 128, TE, out_ref, out_hbm, out_sems)


def backward_kernel(x_ref, table_ref, out_hbm, re_ref, im_ref, conv_ref, out_ref, sems):
    def first(d):
        scale = decode_scale(x_ref[d, 80:88, :])
        for i in range(5):
            lre, lim = decode_pair(x_ref[d, 16 * i : 16 * i + 16, :])
            put(re_ref, im_ref, i, slot(d), (lre * scale, lim * scale))

    repeat(128, first, TD)

    def second(i):
        transform_128(re_ref, im_ref, i, 1)

    repeat(5, second)

    def third(m):
        at = place(m)
        u0 = get(re_ref, im_ref, 0, at)[0]
        z = [times_conj(get(re_ref, im_ref, i, at), table_ref[16 * m + i], table_ref[16 * m + 8 + i]) for i in range(1, 4)]
        re4, im4 = get(re_ref, im_ref, 4, at)
        u4 = re4 * table_ref[16 * m + 4] + im4 * table_ref[16 * m + 12]
        (x1, y1), (x2, y2), (x3, y3) = z
        even, odd = u0 + u4, u0 - u4
        x13, y13 = x1 + x3, y1 - y3
        up, down = even + x2, even - x2
        conv_ref[0, m] = up + x13
        conv_ref[4, m] = up - x13
        conv_ref[2, m] = down - y13
        conv_ref[6, m] = down + y13
        aa, bb = (x1 - x3) * half_root, (y1 + y3) * half_root
        up, down = odd + y2, odd - y2
        diff, both = aa - bb, aa + bb
        conv_ref[1, m] = down + diff
        conv_ref[5, m] = down - diff
        conv_ref[3, m] = up - both
        conv_ref[7, m] = up + both

    repeat(128, third)

    def fourth(step):
        r, g = step // 4, step % 4
        blocks = [conv_ref[r, 32 * g + k] * (1.0 / 1048576.0) for k in range(32)]

        def store(rows, v):
            out_ref[r, g, rows, :] = v

        encode(blocks, store)

    send_parts(fourth, 32, 8, out_ref, out_hbm, sems)


def gate_kernel(x_ref, value_ref, gate_ref, skip_ref, out_ref):
    skip = skip_ref[0:1, :]

    def body(at):
        g, k = at // 16, at % 16
        start = pl.multiple_of(16 * k, 16)
        for pair in range(4):
            sides = []
            for r in (2 * pair, 2 * pair + 1):
                scale = decode_scale(x_ref[r, g, 256:264, :])
                low, high = decode_pair(x_ref[r, g, pl.ds(start, 16), :])
                sides.append((low * scale, high * scale))
            for odd in range(2):
                conv = jnp.concatenate([sides[0][odd], sides[1][odd]], axis=0)
                rows = slice(16 * pair, 16 * pair + 16)
                v = value_ref[2 * at + odd, rows, :].astype(f32)
                w = gate_ref[2 * at + odd, rows, :].astype(f32)
                out_ref[2 * at + odd, rows, :] = (w * (conv + skip * v)).astype(bf16)

    repeat(64 // GS, body, TG)


def roots_table(period):
    m, i = np.arange(128)[:, None], np.arange(8)[None, :]
    angle = -2.0 * np.pi * (m * i % period) / period
    return np.concatenate([np.cos(angle), np.sin(angle)], axis=1).astype(np.float32).reshape(-1)


def wide_roots():
    e, j, c = np.arange(16)[:, None, None], np.arange(8)[None, :, None], np.arange(8)[None, None, :]
    angle = -2.0 * np.pi * (j * (c + 8 * e) % 1024) / 1024
    both = np.stack([np.cos(angle), np.sin(angle)]).astype(np.float32)
    return np.broadcast_to(both[..., None], (2, 16, 8, 8, 128))


def twist_tables(device):
    unit = -2.0 * math.pi / 1048576.0
    source = lax.broadcasted_iota(jnp.int32, (128, 16), 0)
    i = lax.broadcasted_iota(jnp.int32, (128, 16), 1)
    angle = ((64 * (source % 16) + 8 * (source // 16)) * (8 * device + i % 8) % 1048576).astype(f32) * unit
    far = jnp.where(i < 8, jnp.cos(angle), jnp.sin(angle)).reshape(-1)
    shape = (8, 8, 128)
    kp = 8 * device + lax.broadcasted_iota(jnp.int32, shape, 0)
    angle = (kp * lax.broadcasted_iota(jnp.int32, shape, 1)).astype(f32) * unit
    return far, jnp.stack([jnp.cos(angle), jnp.sin(angle)])


def vspec():
    return pl.BlockSpec(memory_space=pltpu.VMEM)


def sspec():
    return pl.BlockSpec(memory_space=pltpu.SMEM)


def aspec():
    return pl.BlockSpec(memory_space=pl.ANY)


def params(mib=56):
    return pltpu.CompilerParams(vmem_limit_bytes=mib * 1024 * 1024)


def forward(columns, table):
    return pl.pallas_call(
        forward_kernel,
        out_shape=jax.ShapeDtypeStruct((128, 88, 128), bf16),
        in_specs=[vspec(), sspec()],
        out_specs=aspec(),
        scratch_shapes=[pltpu.VMEM((5 * STR, 128), f32)] * 2
        + [pltpu.VMEM((128, 88, 128), bf16), pltpu.SemaphoreType.DMA((4,))],
        compiler_params=params(16),
        name="forward_columns",
    )(columns, table)


def leave(value, filter_real, filter_imag):
    return pl.pallas_call(
        leave_kernel,
        out_shape=[jax.ShapeDtypeStruct((8, 64, 16, 128), bf16), jax.ShapeDtypeStruct((8, 3, 264, 128), bf16)],
        in_specs=[aspec()] * 3,
        out_specs=[vspec()] * 2,
        scratch_shapes=[pltpu.VMEM((128, 64, 128), bf16)]
        + [pltpu.VMEM((8192, 128), f32)] * 2
        + [pltpu.SemaphoreType.DMA((17,))],
        compiler_params=params(LV),
        cost_estimate=pl.CostEstimate(flops=8000000, bytes_accessed=14 << 20, transcendentals=1000000),
        name="leave",
    )(value, filter_real, filter_imag)


def merged(filter_real, filter_imag, codes):
    rows = pl.BlockSpec((1024, 128), lambda g: (g, 0))
    return pl.pallas_call(
        merge_kernel,
        grid=(8,),
        out_shape=[jax.ShapeDtypeStruct((8192, 128), f32)] * 2,
        in_specs=[rows, rows, pl.BlockSpec((1, 3, 264, 128), lambda g: (7 - g, 0, 0, 0))],
        out_specs=[rows, rows],
        scratch_shapes=[pltpu.VMEM((1024, 128), f32)] * 2,
        compiler_params=params(),
        cost_estimate=pl.CostEstimate(flops=80000000000, bytes_accessed=18 << 20, transcendentals=0),
        name="merge_filters",
    )(filter_real, filter_imag, codes)


def middle(arrived, far, near, filter_real, filter_imag, roots):
    return pl.pallas_call(
        middle_kernel,
        out_shape=jax.ShapeDtypeStruct((128, 88, 128), bf16),
        in_specs=[vspec(), sspec(), vspec(), aspec(), aspec(), vspec()],
        out_specs=aspec(),
        scratch_shapes=[pltpu.VMEM((5 * STR, 128), f32)] * 4
        + [pltpu.VMEM((128, 5, 8, 128), f32)] * 2
        + [pltpu.VMEM((8192, 128), f32)] * 2
        + [pltpu.VMEM((128, 88, 128), bf16)]
        + [pltpu.SemaphoreType.DMA((2,)), pltpu.SemaphoreType.DMA((4,))],
        compiler_params=params(50),
        name="filter_rows",
    )(arrived, far, near, filter_real, filter_imag, roots)


def backward(returned, table):
    return pl.pallas_call(
        backward_kernel,
        out_shape=jax.ShapeDtypeStruct((8, 4, 264, 128), bf16),
        in_specs=[vspec(), sspec()],
        out_specs=aspec(),
        scratch_shapes=[pltpu.VMEM((5 * STR, 128), f32)] * 2 + [pltpu.VMEM((8, 128, 8, 128), f32)]
        + [pltpu.VMEM((8, 4, 264, 128), bf16), pltpu.SemaphoreType.DMA((4,))],
        compiler_params=params(24),
        name="backward_columns",
    )(returned, table)


def gating(settled, value, gate, skip):
    return pl.pallas_call(
        gate_kernel,
        grid=(GS,),
        out_shape=jax.ShapeDtypeStruct((128, 64, 128), bf16),
        in_specs=[
            pl.BlockSpec((8, 4 // GS, 264, 128), lambda g: (0, g, 0, 0)),
            pl.BlockSpec((128 // GS, 64, 128), lambda g: (g, 0, 0)),
            pl.BlockSpec((128 // GS, 64, 128), lambda g: (g, 0, 0)),
            pl.BlockSpec((1, 128), lambda g: (0, 0)),
        ],
        out_specs=pl.BlockSpec((128 // GS, 64, 128), lambda g: (g, 0, 0)),
        compiler_params=params(16),
        name="gating",
    )(settled, value, gate, skip.reshape(1, 128))


def convolve(value, gate, filter_real, filter_imag, skip):
    device = lax.axis_index("row") * 16 + lax.axis_index("col")
    everyone = ("row", "col")
    table = jnp.asarray(roots_table(1024))
    filter_real = filter_real.reshape(8192, 128)
    filter_imag = filter_imag.reshape(8192, 128)
    pieces, codes = leave(value, filter_real, filter_imag)
    columns = lax.all_to_all(pieces, "row", split_axis=0, concat_axis=0, tiled=True)
    columns, codes = lax.optimization_barrier((columns, codes))
    codes = lax.ppermute(codes, everyone, [(d, 127 - d) for d in range(128)])
    spectrum = forward(columns.reshape(512, 16, 128), table)
    spectrum, device = lax.optimization_barrier((spectrum, device))
    far, near = twist_tables(device)
    arrived = lax.all_to_all(spectrum, everyone, split_axis=0, concat_axis=0, tiled=True)
    both_real, both_imag = merged(filter_real, filter_imag, codes)
    leaving = middle(arrived, far, near, both_real, both_imag, jnp.asarray(wide_roots()))
    returned = lax.all_to_all(leaving, everyone, split_axis=0, concat_axis=0, tiled=True)
    convolved = backward(returned, table)
    settled = lax.all_to_all(convolved, "row", split_axis=0, concat_axis=0, tiled=True)
    return gating(settled, value, gate, skip)


def solution(mesh):
    return jax.shard_map(
        convolve,
        mesh=mesh,
        in_specs=(
            P("row", "col", None),
            P("row", "col", None),
            P(None, ("row", "col"), None),
            P(None, ("row", "col"), None),
            P(),
        ),
        out_specs=P("row", "col", None),
        check_vma=False,
    )
```

```python
import math

import jax
import jax.numpy as jnp
import numpy as np
from jax import lax
from jax.experimental import pallas as pl
from jax.experimental.pallas import tpu as pltpu
from jax.sharding import PartitionSpec as P

GS = 2
TG = 4
LV = 56
TM = 1
TE = 16
TD = 16
half_root = math.sqrt(0.5)
span = 124.0
ln2 = math.log(2.0)
f32 = jnp.float32
bf16 = jnp.bfloat16


def turn(x, sign):
    re, im = x
    return (-im, re) if sign > 0 else (im, -re)


def add(x, y):
    return (x[0] + y[0], x[1] + y[1])


def sub(x, y):
    return (x[0] - y[0], x[1] - y[1])


def scale_root(x, index, period, sign):
    index %= period
    if index == 0:
        return x
    if 4 * index == period:
        return turn(x, sign)
    if 2 * index == period:
        return (-x[0], -x[1])
    re, im = x
    if 8 * index == period:
        if sign > 0:
            return ((re - im) * half_root, (im + re) * half_root)
        return ((re + im) * half_root, (im - re) * half_root)
    if 8 * index == 3 * period:
        if sign > 0:
            return ((re + im) * -half_root, (re - im) * half_root)
        return ((im - re) * half_root, (re + im) * -half_root)
    angle = 2.0 * math.pi * index / period
    c, s = math.cos(angle), sign * math.sin(angle)
    return (re * c - im * s, re * s + im * c)


def times(x, c, s):
    re, im = x
    return (re * c - im * s, re * s + im * c)


def times_conj(x, c, s):
    re, im = x
    return (re * c + im * s, im * c - re * s)


def dft4(y, sign):
    t0, t1 = add(y[0], y[2]), sub(y[0], y[2])
    t2, t3 = add(y[1], y[3]), turn(sub(y[1], y[3]), sign)
    return [add(t0, t2), add(t1, t3), sub(t0, t2), sub(t1, t3)]


def dft8(x, sign):
    even = dft4([add(x[k], x[k + 4]) for k in range(4)], sign)
    odd = dft4([scale_root(sub(x[k], x[k + 4]), k, 8, sign) for k in range(4)], sign)
    return [even[0], odd[0], even[1], odd[1], even[2], odd[2], even[3], odd[3]]


def dft16(x, sign):
    first = [dft4([x[4 * a + b] for a in range(4)], sign) for b in range(4)]
    out = [None] * 16
    for c in range(4):
        last = dft4([scale_root(first[b][c], b * c, 16, sign) for b in range(4)], sign)
        for e in range(4):
            out[c + 4 * e] = last[e]
    return out


STR = 1096


def rows_of(i, at):
    start = i * STR + at * 8
    if STR % 8 == 0 and not isinstance(start, int):
        start = pl.multiple_of(start, 8)
    return pl.ds(start, 8)


def get(re_ref, im_ref, i, at):
    rows = rows_of(i, at)
    return (re_ref[rows, :], im_ref[rows, :])


def put(re_ref, im_ref, i, at, x):
    rows = rows_of(i, at)
    re_ref[rows, :] = x[0]
    im_ref[rows, :] = x[1]


def transform_128(re_ref, im_ref, i, sign):
    for b in range(16):
        x = dft8([get(re_ref, im_ref, i, 17 * a + b) for a in range(8)], sign)
        for c in range(8):
            put(re_ref, im_ref, i, 17 * c + b, scale_root(x[c], b * c, 128, sign))
    for c in range(8):
        x = dft16([get(re_ref, im_ref, i, 17 * c + b) for b in range(16)], sign)
        for e in range(16):
            put(re_ref, im_ref, i, 17 * c + e, x[e])


def repeat(count, step, together=1):
    def body(k, carry):
        for u in range(together):
            step(together * k + u)
        return carry

    lax.fori_loop(0, count // together, body, 0)


def slot(n):
    return 17 * (n // 16) + n % 16


def place(k):
    return 17 * (k % 8) + k // 8


def send_parts(step, count, together, src_ref, dst_ref, sems):
    size = src_ref.shape[0] // 4

    def copy(k):
        rows = pl.ds(size * k, size)
        return pltpu.make_async_copy(src_ref.at[rows], dst_ref.at[rows], sems.at[k])

    def part(k, carry):
        repeat(count // 4, lambda n: step(count // 4 * k + n), together)
        copy(k).start()
        return carry

    lax.fori_loop(0, 4, part, 0)
    for k in range(4):
        copy(k).wait()


def encode(blocks, store):
    tops = [jnp.abs(x) for x in blocks]
    while len(tops) > 1:
        tops = [jnp.maximum(x, y) for x, y in zip(tops[::2], tops[1::2])] + tops[len(tops) // 2 * 2 :]
    scale = jnp.maximum(tops[0] * (1.0 / span), 1e-35).astype(bf16)
    inverse = 1.0 / scale.astype(f32)
    for k in range(len(blocks) // 2):
        pair = jnp.concatenate([blocks[2 * k] * inverse, blocks[2 * k + 1] * inverse], axis=0)
        store(slice(16 * k, 16 * k + 16), jnp.exp2(pair).astype(bf16))
    store(slice(8 * len(blocks), 8 * len(blocks) + 8), scale)


def decode_scale(rows):
    return rows.astype(f32) * (1.0 / ln2)


def decode_pair(rows):
    logs = jnp.log(rows.astype(f32))
    return logs[0:8], logs[8:16]


def forward_kernel(x_ref, table_ref, out_hbm, re_ref, im_ref, out_ref, sems):
    def first(pair):
        both = [x_ref[64 * r + pair].astype(f32) for r in range(8)]
        for odd in range(2):
            m = 2 * pair + odd
            at = slot(m)
            x = [v[8 * odd : 8 * odd + 8] for v in both]
            s = [x[k] + x[k + 4] for k in range(4)]
            d = [x[k] - x[k + 4] for k in range(4)]
            s02, s13 = s[0] + s[2], s[1] + s[3]
            put(re_ref, im_ref, 0, at, (s02 + s13, jnp.zeros_like(s02)))
            low, high = (d[1] - d[3]) * half_root, (d[1] + d[3]) * half_root
            rows = [None, (d[0] + low, -d[2] - high), (s[0] - s[2], s[3] - s[1]), (d[0] - low, d[2] - high)]
            for i in range(1, 4):
                put(re_ref, im_ref, i, at, times(rows[i], table_ref[16 * m + i], table_ref[16 * m + 8 + i]))
            mid = s02 - s13
            put(re_ref, im_ref, 4, at, (mid * table_ref[16 * m + 4], mid * table_ref[16 * m + 12]))

    repeat(64, first)

    def second(i):
        transform_128(re_ref, im_ref, i, -1)

    repeat(5, second)

    def third(d):
        blocks = []
        for i in range(5):
            blocks += get(re_ref, im_ref, i, place(d))

        def store(rows, v):
            out_ref[d, rows, :] = v

        encode(blocks, store)

    send_parts(third, 128, TE, out_ref, out_hbm, sems)


def leave_kernel(value_hbm, real_hbm, imag_hbm, out_ref, code_ref, value_ref, re_ref, im_ref, sems):
    copies = [pltpu.make_async_copy(value_hbm, value_ref, sems.at[0])]
    for g in range(8):
        rows = pl.ds(1024 * g, 1024)
        copies.append(pltpu.make_async_copy(real_hbm.at[rows], re_ref.at[rows], sems.at[1 + g]))
        copies.append(pltpu.make_async_copy(imag_hbm.at[rows], im_ref.at[rows], sems.at[9 + g]))
    for c in copies:
        c.start()
    copies[0].wait()

    def first(k):
        for pair in range(4):
            rows = slice(16 * pair, 16 * pair + 16)
            low, high = value_ref[2 * k, rows, :].astype(f32), value_ref[2 * k + 1, rows, :].astype(f32)
            for odd in range(2):
                half = slice(8 * odd, 8 * odd + 8)
                out_ref[2 * pair + odd, k] = jnp.concatenate([low[half], high[half]], axis=0).astype(bf16)

    repeat(64, first, 8)
    for g in range(8):
        copies[1 + 2 * g].wait()
        copies[2 + 2 * g].wait()
        for s in range(3):
            blocks = []
            for u in range(16):
                rows = pl.ds(1024 * g + 64 * u + 7 - s, 8, stride=8)
                blocks += [re_ref[rows, :], im_ref[rows, :]]

            def store(rows, v, g=g, s=s):
                code_ref[g, s, rows, :] = v

            encode(blocks, store)


def merge_kernel(re_ref, im_ref, code_ref, out_re, out_im, far_re, far_im):
    far_re[...] = jnp.zeros((1024, 128), f32)
    far_im[...] = jnp.zeros((1024, 128), f32)
    for s in range(3):
        scale = decode_scale(code_ref[0, s, 256:264, :])
        for u in range(16):
            lre, lim = decode_pair(code_ref[0, s, 16 * u : 16 * u + 16, :])
            rows = pl.ds(64 * u + s + 1, 8, stride=8)
            far_re[rows, :] = lre * scale
            far_im[rows, :] = lim * scale
    for t in range(128):
        here, there = slice(8 * t, 8 * t + 8), slice(1016 - 8 * t, 1024 - 8 * t)
        out_re[here, :] = re_ref[here, :] + far_re[there, :]
        out_im[here, :] = im_ref[here, :] - far_im[there, :]


def middle_kernel(x_ref, far_ref, near_ref, filter_real, filter_imag, root_ref, out_ref,
                  re_ref, im_ref, re2_ref, im2_ref, tc_ref, ts_ref, fr_ref, fi_ref, sems):
    copies = [
        pltpu.make_async_copy(filter_real, fr_ref, sems.at[0]),
        pltpu.make_async_copy(filter_imag, fi_ref, sems.at[1]),
    ]
    for c in copies:
        c.start()

    def first(src):
        a = 8 * (src % 16) + src // 16
        scale = decode_scale(x_ref[src, 80:88, :])
        for i in range(5):
            x = decode_pair(x_ref[src, 16 * i : 16 * i + 16, :])
            c, s = times((near_ref[0, i], near_ref[1, i]), far_ref[16 * src + i], far_ref[16 * src + 8 + i])
            tc_ref[src, i] = c
            ts_ref[src, i] = s
            put(re_ref, im_ref, i, slot(a), times(x, scale * c, scale * s))

    repeat(128, first, TD)

    def second(i):
        transform_128(re_ref, im_ref, i, -1)

    repeat(5, second)
    for c in copies:
        c.wait()

    def third(e):
        start = 136 * (e // 2) + 64 * (e % 2)
        for i in range(5):
            x = []
            for j in range(8):
                rows = pl.ds(i * STR + 8 * e + j, 8, stride=136)
                x.append((re_ref[rows, :], im_ref[rows, :]))
            for j in range(1, 8):
                x[j] = times(x[j], root_ref[0, e, j], root_ref[1, e, j])
            x = dft8(x, -1)
            y = []
            for k in range(8):
                rows = pl.ds(64 * e + 1024 * k + i, 8, stride=8)
                y.append(times(x[k], fr_ref[rows, :], fi_ref[rows, :]))
            y = dft8(y, 1)
            for j in range(8):
                if j:
                    y[j] = times_conj(y[j], root_ref[0, e, j], root_ref[1, e, j])
                rows = pl.ds(i * STR + start + j, 8, stride=8)
                re2_ref[rows, :] = y[j][0]
                im2_ref[rows, :] = y[j][1]

    repeat(16, third, TM)

    def fourth(i):
        transform_128(re2_ref, im2_ref, i, 1)

    repeat(5, fourth)

    def fifth(src):
        a = 8 * (src % 16) + src // 16
        blocks = []
        for i in range(5):
            blocks += times_conj(get(re2_ref, im2_ref, i, place(a)), tc_ref[src, i], ts_ref[src, i])

        def store(rows, v):
            out_ref[src, rows, :] = v

        encode(blocks, store)

    repeat(128, fifth, TE)


def backward_kernel(x_ref, table_ref, out_ref, re_ref, im_ref, conv_ref):
    def first(d):
        scale = decode_scale(x_ref[d, 80:88, :])
        for i in range(5):
            lre, lim = decode_pair(x_ref[d, 16 * i : 16 * i + 16, :])
            put(re_ref, im_ref, i, slot(d), (lre * scale, lim * scale))

    repeat(128, first, TD)

    def second(i):
        transform_128(re_ref, im_ref, i, 1)

    repeat(5, second)

    def third(m):
        at = place(m)
        u0 = get(re_ref, im_ref, 0, at)[0]
        z = [times_conj(get(re_ref, im_ref, i, at), table_ref[16 * m + i], table_ref[16 * m + 8 + i]) for i in range(1, 4)]
        re4, im4 = get(re_ref, im_ref, 4, at)
        u4 = re4 * table_ref[16 * m + 4] + im4 * table_ref[16 * m + 12]
        (x1, y1), (x2, y2), (x3, y3) = z
        even, odd = u0 + u4, u0 - u4
        x13, y13 = x1 + x3, y1 - y3
        up, down = even + x2, even - x2
        conv_ref[0, m] = up + x13
        conv_ref[4, m] = up - x13
        conv_ref[2, m] = down - y13
        conv_ref[6, m] = down + y13
        aa, bb = (x1 - x3) * half_root, (y1 + y3) * half_root
        up, down = odd + y2, odd - y2
        diff, both = aa - bb, aa + bb
        conv_ref[1, m] = down + diff
        conv_ref[5, m] = down - diff
        conv_ref[3, m] = up - both
        conv_ref[7, m] = up + both

    repeat(128, third)

    def fourth(step):
        r, g = step // 4, step % 4
        blocks = [conv_ref[r, 32 * g + k] * (1.0 / 1048576.0) for k in range(32)]

        def store(rows, v):
            out_ref[r, g, rows, :] = v

        encode(blocks, store)

    repeat(32, fourth, 8)


def gate_kernel(x_ref, value_ref, gate_ref, skip_ref, out_ref):
    skip = skip_ref[0:1, :]

    def body(at):
        g, k = at // 16, at % 16
        start = pl.multiple_of(16 * k, 16)
        for pair in range(4):
            sides = []
            for r in (2 * pair, 2 * pair + 1):
                scale = decode_scale(x_ref[r, g, 256:264, :])
                low, high = decode_pair(x_ref[r, g, pl.ds(start, 16), :])
                sides.append((low * scale, high * scale))
            for odd in range(2):
                conv = jnp.concatenate([sides[0][odd], sides[1][odd]], axis=0)
                rows = slice(16 * pair, 16 * pair + 16)
                v = value_ref[2 * at + odd, rows, :].astype(f32)
                w = gate_ref[2 * at + odd, rows, :].astype(f32)
                out_ref[2 * at + odd, rows, :] = (w * (conv + skip * v)).astype(bf16)

    repeat(64 // GS, body, TG)


def roots_table(period):
    m, i = np.arange(128)[:, None], np.arange(8)[None, :]
    angle = -2.0 * np.pi * (m * i % period) / period
    return np.concatenate([np.cos(angle), np.sin(angle)], axis=1).astype(np.float32).reshape(-1)


def wide_roots():
    e, j, c = np.arange(16)[:, None, None], np.arange(8)[None, :, None], np.arange(8)[None, None, :]
    angle = -2.0 * np.pi * (j * (c + 8 * e) % 1024) / 1024
    both = np.stack([np.cos(angle), np.sin(angle)]).astype(np.float32)
    return np.broadcast_to(both[..., None], (2, 16, 8, 8, 128))


def twist_tables(device):
    unit = -2.0 * math.pi / 1048576.0
    source = lax.broadcasted_iota(jnp.int32, (128, 16), 0)
    i = lax.broadcasted_iota(jnp.int32, (128, 16), 1)
    angle = ((64 * (source % 16) + 8 * (source // 16)) * (8 * device + i % 8) % 1048576).astype(f32) * unit
    far = jnp.where(i < 8, jnp.cos(angle), jnp.sin(angle)).reshape(-1)
    shape = (8, 8, 128)
    kp = 8 * device + lax.broadcasted_iota(jnp.int32, shape, 0)
    angle = (kp * lax.broadcasted_iota(jnp.int32, shape, 1)).astype(f32) * unit
    return far, jnp.stack([jnp.cos(angle), jnp.sin(angle)])


def vspec():
    return pl.BlockSpec(memory_space=pltpu.VMEM)


def sspec():
    return pl.BlockSpec(memory_space=pltpu.SMEM)


def aspec():
    return pl.BlockSpec(memory_space=pl.ANY)


def params(mib=56):
    return pltpu.CompilerParams(vmem_limit_bytes=mib * 1024 * 1024)


def forward(columns, table):
    return pl.pallas_call(
        forward_kernel,
        out_shape=jax.ShapeDtypeStruct((128, 88, 128), bf16),
        in_specs=[vspec(), sspec()],
        out_specs=aspec(),
        scratch_shapes=[pltpu.VMEM((5 * STR, 128), f32)] * 2
        + [pltpu.VMEM((128, 88, 128), bf16), pltpu.SemaphoreType.DMA((4,))],
        compiler_params=params(16),
        name="forward_columns",
    )(columns, table)


def leave(value, filter_real, filter_imag):
    return pl.pallas_call(
        leave_kernel,
        out_shape=[jax.ShapeDtypeStruct((8, 64, 16, 128), bf16), jax.ShapeDtypeStruct((8, 3, 264, 128), bf16)],
        in_specs=[aspec()] * 3,
        out_specs=[vspec()] * 2,
        scratch_shapes=[pltpu.VMEM((128, 64, 128), bf16)]
        + [pltpu.VMEM((8192, 128), f32)] * 2
        + [pltpu.SemaphoreType.DMA((17,))],
        compiler_params=params(LV),
        cost_estimate=pl.CostEstimate(flops=8000000, bytes_accessed=14 << 20, transcendentals=1000000),
        name="leave",
    )(value, filter_real, filter_imag)


def merged(filter_real, filter_imag, codes):
    rows = pl.BlockSpec((1024, 128), lambda g: (g, 0))
    return pl.pallas_call(
        merge_kernel,
        grid=(8,),
        out_shape=[jax.ShapeDtypeStruct((8192, 128), f32)] * 2,
        in_specs=[rows, rows, pl.BlockSpec((1, 3, 264, 128), lambda g: (7 - g, 0, 0, 0))],
        out_specs=[rows, rows],
        scratch_shapes=[pltpu.VMEM((1024, 128), f32)] * 2,
        compiler_params=params(),
        cost_estimate=pl.CostEstimate(flops=80000000000, bytes_accessed=18 << 20, transcendentals=0),
        name="merge_filters",
    )(filter_real, filter_imag, codes)


def middle(arrived, far, near, filter_real, filter_imag, roots):
    return pl.pallas_call(
        middle_kernel,
        out_shape=jax.ShapeDtypeStruct((128, 88, 128), bf16),
        in_specs=[vspec(), sspec(), vspec(), aspec(), aspec(), vspec()],
        out_specs=vspec(),
        scratch_shapes=[pltpu.VMEM((5 * STR, 128), f32)] * 4
        + [pltpu.VMEM((128, 5, 8, 128), f32)] * 2
        + [pltpu.VMEM((8192, 128), f32)] * 2
        + [pltpu.SemaphoreType.DMA((2,))],
        compiler_params=params(50),
        name="filter_rows",
    )(arrived, far, near, filter_real, filter_imag, roots)


def backward(returned, table):
    return pl.pallas_call(
        backward_kernel,
        out_shape=jax.ShapeDtypeStruct((8, 4, 264, 128), bf16),
        in_specs=[vspec(), sspec()],
        out_specs=vspec(),
        scratch_shapes=[pltpu.VMEM((5 * STR, 128), f32)] * 2 + [pltpu.VMEM((8, 128, 8, 128), f32)],
        compiler_params=params(24),
        name="backward_columns",
    )(returned, table)


def gating(settled, value, gate, skip):
    return pl.pallas_call(
        gate_kernel,
        grid=(GS,),
        out_shape=jax.ShapeDtypeStruct((128, 64, 128), bf16),
        in_specs=[
            pl.BlockSpec((8, 4 // GS, 264, 128), lambda g: (0, g, 0, 0)),
            pl.BlockSpec((128 // GS, 64, 128), lambda g: (g, 0, 0)),
            pl.BlockSpec((128 // GS, 64, 128), lambda g: (g, 0, 0)),
            pl.BlockSpec((1, 128), lambda g: (0, 0)),
        ],
        out_specs=pl.BlockSpec((128 // GS, 64, 128), lambda g: (g, 0, 0)),
        compiler_params=params(16),
        name="gating",
    )(settled, value, gate, skip.reshape(1, 128))


def convolve(value, gate, filter_real, filter_imag, skip):
    device = lax.axis_index("row") * 16 + lax.axis_index("col")
    everyone = ("row", "col")
    table = jnp.asarray(roots_table(1024))
    filter_real = filter_real.reshape(8192, 128)
    filter_imag = filter_imag.reshape(8192, 128)
    pieces, codes = leave(value, filter_real, filter_imag)
    columns = lax.all_to_all(pieces, "row", split_axis=0, concat_axis=0, tiled=True)
    columns, codes = lax.optimization_barrier((columns, codes))
    codes = lax.ppermute(codes, everyone, [(d, 127 - d) for d in range(128)])
    spectrum = forward(columns.reshape(512, 16, 128), table)
    spectrum, device = lax.optimization_barrier((spectrum, device))
    far, near = twist_tables(device)
    arrived = lax.all_to_all(spectrum, everyone, split_axis=0, concat_axis=0, tiled=True)
    both_real, both_imag = merged(filter_real, filter_imag, codes)
    leaving = middle(arrived, far, near, both_real, both_imag, jnp.asarray(wide_roots()))
    returned = lax.all_to_all(leaving, everyone, split_axis=0, concat_axis=0, tiled=True)
    convolved = backward(returned, table)
    settled = lax.all_to_all(convolved, "row", split_axis=0, concat_axis=0, tiled=True)
    return gating(settled, value, gate, skip)


def solution(mesh):
    return jax.shard_map(
        convolve,
        mesh=mesh,
        in_specs=(
            P("row", "col", None),
            P("row", "col", None),
            P(None, ("row", "col"), None),
            P(None, ("row", "col"), None),
            P(),
        ),
        out_specs=P("row", "col", None),
        check_vma=False,
    )
```
